32 devices in a mesh: reorder: 4 (over z), pair: 8 (over y, x, core).
Axes of the slice: x: 2, y: 2, z: 4, core: 2. Of those that a mesh axis runs over, the one named last changes fastest.
Arguments:
- amps: bfloat16 [8, 8, 16, 4096], P('pair', 'reorder'), may hold values from -3 to 3
- tile_index: int32 [8, 8, 16], replicated, may hold values from 0 to 625, as said below
- ovov: bfloat16 [8, 8, 16, 4096], P('pair', 'reorder'), may hold values from -6 to 6
- cycle_ints: bfloat16 [8, 8, 25, 25, 4096], P('pair', 'reorder'), may hold values from -0.375 to 0.375
- history: bfloat16 [6, 8, 8, 16, 4096], P(None, 'pair', 'reorder'), may hold values from -6 to 6
- slab: int32 [8], replicated, may hold values from 0 to 199, as said below
- eps_occ: float32 [200], replicated, may hold values from -2 to -0.5
- eps_vir: float32 [1600], replicated, may hold values from 0.3 to 4
Outputs:
- new_amps: bfloat16 [8, 8, 16, 4096], P('pair', 'reorder')
- gram_row: float32 [7], replicated
The draws below stay inside these ranges and needn't reach their ends.
Inputs may be any that keep to these rules, and one draw needn't show every extreme that they name: `tile_index`: entry (i, j, s) is a * 25 + b for the distinct tile (a, b) held in slot s of pair (i, j), or 625 for an empty slot. Live slots come first; each pair has 2 or more. At most 2 live tiles of one pair share a row a, reached. Pairs (i, 2m) and (i, 2m + 1) hold at most 24 live tiles together, reached; some pair holds 16. `slab`: distinct occupied orbitals.
All inputs are finite; a program needn't handle non-finite values.
Results may differ from the reference program's by a relative error of at most 0.008.
Values may be sent and summed in bfloat16 or wider, within the bound.
No kernel may reach another device: no remote copies, remote signals or barrier semaphores. Data moves between devices by JAX's collectives and lax.ppermute only.
A program may use at most 128 MiB of HBM per device.

```python
import jax
import jax.numpy as jnp
from jax import lax

V = 1600
NOCC = 200
TILE = 64
NT = 25
NS = 8
CAPT = 16
ROWCAP = 2
LIVE2 = 24
NHIST = 6


def draw_tile_index(key, part):
    key = jax.random.fold_in(key, 11)
    across = V // TILE
    key_rows, key_cols, key_order, key_first, key_second, key_pick = jax.random.split(key, 6)
    pairs = NS * NS
    rows = jax.vmap(lambda k: jax.random.permutation(k, across)[:CAPT // ROWCAP])(jax.random.split(key_rows, pairs))
    rows = jnp.repeat(rows, ROWCAP, axis=1)
    cols = jax.vmap(lambda k: jax.random.permutation(k, across)[:CAPT])(jax.random.split(key_cols, pairs))
    order = jax.vmap(lambda k: jax.random.permutation(k, CAPT))(jax.random.split(key_order, pairs))
    tiles = jnp.take_along_axis(rows * across + cols, order, axis=1).reshape(NS, NS, CAPT)
    half = NS // 2
    first = jax.random.randint(key_first, (NS, half), 2, CAPT + 1)
    second_top = jnp.minimum(CAPT, LIVE2 - first) + 1
    second = jax.random.randint(key_second, (NS, half), 2, second_top)
    chosen = jax.random.randint(key_pick, (), 0, NS * half)
    places = jnp.arange(NS * half).reshape(NS, half)
    first = jnp.where(places == chosen, CAPT, first)
    second = jnp.where(places == chosen, LIVE2 - CAPT, second)
    counts = jnp.stack([first, second], axis=2).reshape(NS, NS)
    slot = jnp.arange(CAPT)
    return jnp.where(slot[None, None, :] < counts[..., None], tiles, across * across).astype(jnp.int32)


def draw_slab(key, part):
    key = jax.random.fold_in(key, 23)
    key_inner, key_order = jax.random.split(key, 2)
    inner = jax.random.permutation(key_inner, NOCC - 2)[:NS - 2] + 1
    chosen = jnp.concatenate([jnp.array([0, NOCC - 1], dtype=jnp.int32), inner.astype(jnp.int32)])
    return jax.random.permutation(key_order, chosen).astype(jnp.int32)


def block_levels(own_key, extent, shards, least, largest):
    loudness, own = 1.0, jax.random.fold_in(own_key, 6)
    for position, blocks in shards:
        heights = jnp.exp(jax.random.uniform(jax.random.fold_in(own, position), (blocks,), jnp.float32, least / len(shards), largest / len(shards)))
        loudness = loudness * jnp.repeat(heights, extent[position] // blocks).reshape([-1 if axis == position else 1 for axis in range(len(extent))])
    return loudness


def centred(stream_key, dims, scale, most, pieces=(), held_as=jnp.bfloat16):
    entries = scale * jax.random.normal(stream_key, dims, jnp.float32)
    if pieces:
        entries = entries * block_levels(stream_key, dims, pieces, -0.22, 0.18)
    return jnp.clip(entries, -most, most).astype(held_as)


def setup_inputs(seed: int = 0) -> dict:
    arg_keys = jax.random.split(jax.random.key(seed), 9)
    return {
        "amps": centred(arg_keys[0], (NS, NS, CAPT, TILE * TILE), 0.5, 3.0, ((0, 8), (1, 4))),
        "tile_index": draw_tile_index(jax.random.fold_in(arg_keys[8], 71), 0),
        "ovov": centred(arg_keys[2], (NS, NS, CAPT, TILE * TILE), 1.0, 6.0, ((0, 8), (1, 4))),
        "cycle_ints": centred(arg_keys[3], (NS, NS, NT, NT, TILE * TILE), (TILE * NS // 2) ** -0.5, 0.375, ((0, 8), (1, 4))),
        "history": centred(arg_keys[4], (NHIST, NS, NS, CAPT, TILE * TILE), 1.0, 6.0, ((1, 8), (2, 4))),
        "slab": draw_slab(jax.random.fold_in(arg_keys[8], 71), 0),
        "eps_occ": jnp.clip(jax.random.uniform(arg_keys[6], (NOCC,), jnp.float32, -2.0, -0.5), -2.0, -0.5),
        "eps_vir": jnp.clip(jax.random.uniform(arg_keys[7], (V,), jnp.float32, 0.3, 4.0), 0.3, 4.0),
    }


def match_lists(out_idx, in_idx, across):
    live_in = in_idx < across * across
    same = ((out_idx // across)[:, None] == (in_idx // across)[None, :]) & live_in[None, :]
    width = in_idx.shape[0]
    ranks = width - jnp.arange(width, dtype=jnp.int32)
    scores = jnp.where(same, ranks[None, :], jnp.zeros_like(ranks)[None, :])
    values, picks = lax.top_k(scores, ROWCAP)
    return (picks, values > 0)

def cycle_block(tiles, in_idx, ints_k, out_idx, out_pair):
    across = ints_k.shape[1]
    slots = out_idx.shape[0]
    picks, present = match_lists(out_idx, in_idx, across)
    cols_in = in_idx % across
    cols_out = out_idx % across
    left = tiles[picks].astype(jnp.float32) * present[..., None].astype(jnp.float32)
    left = left.reshape(slots, ROWCAP, TILE, TILE).transpose(0, 2, 1, 3).reshape(slots, TILE, ROWCAP * TILE)
    right = ints_k[out_pair[:, None], cols_in[picks], cols_out[:, None]].astype(jnp.float32)
    right = right.reshape(slots, ROWCAP * TILE, TILE)
    return jnp.einsum('sak,skb->sab', left, right, precision=lax.Precision.HIGHEST)

def reference(amps, tile_index, ovov, cycle_ints, history, slab, eps_occ, eps_vir):
    across = V // TILE
    live = (tile_index < across * across).astype(jnp.float32)
    rows_a = jnp.minimum(tile_index // across, across - 1)
    cols_b = tile_index % across

    def one_pair(flat):
        first = flat // NS
        second = flat % NS
        out_idx = tile_index[first, second]
        out_pair = jnp.zeros((CAPT,), jnp.int32) + second

        def add_term(total, other):
            term = cycle_block(amps[first, other], tile_index[first, other], cycle_ints[other], out_idx, out_pair)
            return (total + term, None)
        start = jnp.zeros((CAPT, TILE, TILE), jnp.float32)
        total, _ = lax.scan(add_term, start, jnp.arange(NS, dtype=jnp.int32))
        return total.reshape(CAPT, TILE * TILE)
    cycle = lax.map(one_pair, jnp.arange(NS * NS, dtype=jnp.int32)).reshape(NS, NS, CAPT, TILE * TILE)
    resid = (ovov.astype(jnp.float32) + cycle) * live[..., None]
    occ_energy = eps_occ[slab]
    vir_tiles = eps_vir.reshape(across, TILE)
    row_energy = vir_tiles[rows_a]
    col_energy = vir_tiles[cols_b]
    denom = occ_energy[:, None, None, None, None] + occ_energy[None, :, None, None, None]
    denom = denom - row_energy[..., :, None] - col_energy[..., None, :]
    denom = denom.reshape(NS, NS, CAPT, TILE * TILE)
    new_amps = ((amps.astype(jnp.float32) + resid / denom) * live[..., None]).astype(jnp.bfloat16)
    cross = jnp.einsum('hijsx,ijsx->h', history.astype(jnp.float32), resid, precision=lax.Precision.HIGHEST)
    square = jnp.sum(resid * resid)
    gram_row = jnp.concatenate([cross, jnp.sqrt(square)[None]]) / (TILE * NS)
    return (new_amps, gram_row)
```

```python
import functools

import jax
import jax.numpy as jnp
from jax import lax
from jax.experimental import pallas as pl
from jax.experimental.pallas import tpu as pltpu
from jax.sharding import PartitionSpec as P

TILE = 64
ROWS = 32
LANES = 128
LIVE2 = 24
F32 = jnp.float32
BF16 = jnp.bfloat16
SMEM = pl.BlockSpec(memory_space=pltpu.SMEM)
VMEM = pl.BlockSpec(memory_space=pltpu.VMEM)


def count_live(ti_ref, i, j, capt, dead):
    total = jnp.int32(0)
    for s in range(capt):
        total = total + (ti_ref[i, j, s] < dead).astype(jnp.int32)
    return total


def row_of(idx, across):
    factor = -(-(1 << 17) // across)
    assert all((n * factor) >> 17 == n // across for n in range(across * across + 1))
    return lax.shift_right_logical(idx * factor, 17)


def pack_kernel(capt, across, ti_ref, amps_ref, out_ref, flat_ref, turned_ref):
    first = lax.axis_index("pair")
    second = lax.axis_index("reorder") * 2
    live1 = count_live(ti_ref, first, second + 1, capt, across * across)
    for jj in range(2):
        for p in range(ROWS):
            chunk = amps_ref[0, jj, :, p * LANES : (p + 1) * LANES].astype(F32)
            for g in range(capt // 8):
                start = (jj * capt + g * 8) * ROWS + p
                flat_ref[pl.ds(start, 8, stride=ROWS), :] = chunk[g * 8 : (g + 1) * 8]
    old = lax.broadcasted_iota(jnp.int32, (LANES, LANES), 0)
    new = lax.broadcasted_iota(jnp.int32, (LANES, LANES), 1)
    source = (new // 64) * 64 + (new % 32) * 2 + (new % 64) // 32
    turn = (old == source).astype(F32).astype(BF16)
    turned_ref[...] = jnp.dot(
        flat_ref[...].astype(BF16), turn, preferred_element_type=F32
    ).astype(BF16)
    out_ref[0:capt] = turned_ref[0 : capt * ROWS].reshape(capt, ROWS, LANES)
    out_ref[capt:LIVE2] = jnp.zeros((LIVE2 - capt, ROWS, LANES), BF16)

    def place(s, carry):
        start = pl.multiple_of((capt + s) * ROWS, ROWS)
        out_ref[LIVE2 - live1 + s] = turned_ref[pl.ds(start, ROWS), :]
        return carry

    lax.fori_loop(0, live1, place, 0)


def pack(amps, ti, capt, across):
    return pl.pallas_call(
        functools.partial(pack_kernel, capt, across),
        in_specs=[SMEM, VMEM],
        out_specs=VMEM,
        scratch_shapes=[
            pltpu.VMEM((2 * capt * ROWS, LANES), F32),
            pltpu.VMEM((2 * capt * ROWS, LANES), BF16),
        ],
        out_shape=jax.ShapeDtypeStruct((LIVE2, ROWS, LANES), BF16),
        cost_estimate=pl.CostEstimate(flops=10**8, bytes_accessed=500000, transcendentals=0),
        name="pack_amps",
    )(ti, amps)


def prep_kernel(
    capt, across, nq, nmax, ti_ref, slab_ref, occ_ref, ints_ref, row_ref, col_ref,
    meta_ref, mine_ref, send_ref, inv_ref, wide_ref, den_ref, tab_ref,
):
    dead = across * across
    me = lax.axis_index("pair")
    sibling = me ^ 1
    plane = lax.axis_index("reorder")
    second = plane * 2

    def build(which, who, k):
        def field(f):
            return (which * 5 + f) * nmax

        parity = lax.rem(k, 2)

        def one_first(q, cnt):
            i = (plane ^ q) * 2 + (who & 1)
            out = (lax.shift_right_logical(who, 1) ^ plane ^ q) * LIVE2
            for a in range(across + 1):
                tab_ref[a] = -1
            live_in = jnp.int32(0)
            for t in range(capt):
                idx = ti_ref[i, k, t]
                live_in = live_in + (idx < dead).astype(jnp.int32)
                a = row_of(idx, across)
                held = t * 32 + idx - a * across
                old = tab_ref[a]
                tab_ref[a] = jnp.where(old < 0, held, old)
                tab_ref[32 + a] = jnp.where(old < 0, -1, held)
            shift = q * LIVE2 + jnp.where(parity == 1, LIVE2 - live_in, 0)
            live1 = count_live(ti_ref, i, second + 1, capt, dead)
            for jj in range(2):
                for s in range(capt):
                    idx = ti_ref[i, second + jj, s]
                    a = row_of(idx, across)
                    b = idx - a * across
                    h0 = tab_ref[a]
                    h1 = tab_ref[32 + a]
                    hit = (idx < dead) & (h0 >= 0)
                    both = h1 >= 0
                    if which < 2:
                        place = out + (s if jj == 0 else LIVE2 - live1 + s)
                        meta_ref[field(0) + cnt] = place
                        t0 = shift + lax.shift_right_arithmetic(h0, 5)
                        t1 = shift + lax.shift_right_arithmetic(h1, 5)
                        meta_ref[field(1) + cnt] = t0
                        meta_ref[field(2) + cnt] = jnp.where(both, t1, t0)
                    if which != 1:
                        w0 = ((h0 & 31) * across + b) * 2 + jj
                        w1 = ((h1 & 31) * across + b) * 2 + jj
                        meta_ref[field(3) + cnt] = w0
                        meta_ref[field(4) + cnt] = jnp.where(both, w1, -1)
                    cnt = cnt + hit.astype(jnp.int32)
            return cnt

        total = lax.fori_loop(0, nq, one_first, jnp.int32(0))
        meta_ref[15 * nmax + which] = total
        return total

    def gather(which, total, tiles_ref):
        def fetch(step, carry):
            for u in range(4):
                e = jnp.minimum(step * 4 + u, total - 1)
                for m in range(2):
                    at = jnp.maximum(meta_ref[(which * 5 + 3 + m) * nmax + e], 0)
                    wide_ref[2 * u + m] = ints_ref[lax.shift_right_logical(at, 1)].astype(F32)
            for u in range(4):
                e = jnp.minimum(step * 4 + u, total - 1)
                for m in range(2):
                    at = meta_ref[(which * 5 + 3 + m) * nmax + e]
                    jj = jnp.maximum(at, 0) & 1
                    tile = wide_ref[2 * u + m, pl.ds(jj, ROWS, stride=2), :]
                    if m == 1:
                        tile = jnp.where(at >= 0, tile, 0.0)
                    tiles_ref[e, m * ROWS : (m + 1) * ROWS] = tile.astype(BF16)
            return carry

        lax.fori_loop(0, (total + 3) // 4, fetch, 0)

    gather(2, build(2, sibling, me), send_ref)
    gather(0, build(0, me, me), mine_ref)
    build(1, me, sibling)

    occ_i = occ_ref[slab_ref[me]]
    for jj in range(2):
        occ = occ_i + occ_ref[slab_ref[second + jj]]

        def denom(s, carry):
            idx = ti_ref[me, second + jj, s]
            row = row_of(idx, across)
            a = jnp.minimum(row, across - 1)
            b = idx - row * across
            at = pl.multiple_of((jj * capt + s) * ROWS, ROWS)
            den_ref[pl.ds(at, ROWS), :] = 1.0 / ((occ - row_ref[a]) - col_ref[b])
            return carry

        lax.fori_loop(0, capt, denom, 0)
        for p in range(ROWS):
            for g in range(capt // 8):
                inv_ref[jj, g * 8 : (g + 1) * 8, p * LANES : (p + 1) * LANES] = den_ref[
                    pl.ds((jj * capt + g * 8) * ROWS + p, 8, stride=ROWS), :
                ]


def prep(cycle_ints, ti, slab, eps_occ, eps_vir, capt, across, nq):
    nmax = nq * LIVE2 + 8
    vir = eps_vir.reshape(across, ROWS, 2, 1)
    row_table = jnp.broadcast_to(vir, (across, ROWS, 2, 64)).reshape(across, ROWS, LANES)
    col_table = jnp.broadcast_to(
        eps_vir.reshape(across, 1, 1, 64), (across, 1, 2, 64)
    ).reshape(across, 1, LANES)
    ints = cycle_ints[0].transpose(1, 2, 0, 3).reshape(across, across, 2, ROWS, LANES)
    ints = ints.transpose(0, 1, 3, 2, 4).reshape(across * across, 2 * ROWS, LANES)
    tiles = jax.ShapeDtypeStruct((nq * LIVE2, 2 * ROWS, LANES), BF16)
    return pl.pallas_call(
        functools.partial(prep_kernel, capt, across, nq, nmax),
        in_specs=[SMEM, SMEM, SMEM, VMEM, VMEM, VMEM],
        out_specs=[SMEM, VMEM, VMEM, VMEM],
        scratch_shapes=[
            pltpu.VMEM((8, 2 * ROWS, LANES), F32),
            pltpu.VMEM((2 * capt * ROWS, LANES), F32),
            pltpu.SMEM((64,), jnp.int32),
        ],
        out_shape=[
            jax.ShapeDtypeStruct((15 * nmax + 8,), jnp.int32),
            tiles,
            tiles,
            jax.ShapeDtypeStruct((2, capt, TILE * TILE), F32),
        ],
        compiler_params=pltpu.CompilerParams(vmem_limit_bytes=32 * 1024 * 1024),
        cost_estimate=pl.CostEstimate(flops=10**9, bytes_accessed=40 * 10**6, transcendentals=0),
        name="prep_integrals",
    )(ti, slab, eps_occ, ints, row_table, col_table)


def multiply_kernel(which, nq, nmax, unroll, meta_ref, tiles_ref, *refs):
    amps_refs, refs = refs[:nq], refs[nq:]
    if which == 0:
        sum_ref, amps_ref = refs
        sum_ref[...] = jnp.zeros(sum_ref.shape, F32)
    else:
        sum_ref, out_refs, amps_ref = refs[0], refs[1:-1], refs[-1]
    for q in range(nq):
        amps_ref[q * LIVE2 : (q + 1) * LIVE2] = amps_refs[q][...]
    low = lax.broadcasted_iota(jnp.int32, (ROWS, LANES), 1) < 64

    def spread(w):
        w = w.astype(F32)
        r = pltpu.roll(w, 64, 1)
        zero = jnp.zeros_like(w)
        parts = [
            jnp.where(low, w, zero),
            jnp.where(low, r, zero),
            jnp.where(low, zero, r),
            jnp.where(low, zero, w),
        ]
        return jnp.concatenate(parts, axis=0).astype(BF16)

    total = meta_ref[15 * nmax + which]

    def several(step, carry):
        results = []
        for u in range(unroll):
            e = jnp.minimum(step * unroll + u, total - 1)
            at = which * 5 * nmax + e
            left = jnp.concatenate(
                [amps_ref[meta_ref[nmax + at]], amps_ref[meta_ref[2 * nmax + at]]], axis=1
            )
            right = jnp.concatenate(
                [spread(tiles_ref[e, 0:ROWS]), spread(tiles_ref[e, ROWS : 2 * ROWS])], axis=0
            )
            place = jnp.where(step * unroll + u < total, meta_ref[at], nq * LIVE2)
            results.append((place, jnp.dot(left, right, preferred_element_type=F32)))
        for place, value in results:
            if which == 0:
                sum_ref[place] = value
            else:
                sum_ref[place] += value
        return carry

    lax.fori_loop(0, (total + unroll - 1) // unroll, several, 0)
    if which == 1:
        for q in range(nq):
            out_refs[q][...] = sum_ref[q * LIVE2 : (q + 1) * LIVE2].astype(BF16)


def multiply(which, meta, tiles, amps, sums, nq):
    block = jax.ShapeDtypeStruct((LIVE2, ROWS, LANES), BF16)
    scratch = [pltpu.VMEM((nq * LIVE2, ROWS, LANES), BF16)]
    if which == 0:
        out = jax.ShapeDtypeStruct((nq * LIVE2 + 1, ROWS, LANES), F32)
    else:
        out = [block] * nq
    return pl.pallas_call(
        functools.partial(multiply_kernel, which, nq, nq * LIVE2 + 8, 8),
        in_specs=[SMEM] + [VMEM] * (1 + nq + len(sums)),
        out_specs=jax.tree.map(lambda _: VMEM, out),
        out_shape=out,
        scratch_shapes=scratch,
        compiler_params=pltpu.CompilerParams(vmem_limit_bytes=24 * 1024 * 1024),
        cost_estimate=pl.CostEstimate(flops=10**9, bytes_accessed=10**7, transcendentals=0),
        name="multiply_own" if which == 0 else "multiply_sibling",
    )(meta, tiles, *amps, *sums)


def update_kernel(
    capt, across, nq, ti_ref, amps_ref, ovov_ref, hist_ref, inv_ref, *refs
):
    part_refs, (new_ref, gram_ref, sum_ref) = refs[:nq], refs[nq:]
    nhist = hist_ref.shape[0]
    first = lax.axis_index("pair")
    second = lax.axis_index("reorder") * 2

    def add(s, carry):
        acc = part_refs[0][s].astype(F32)
        for part_ref in part_refs[1:]:
            acc = acc + part_ref[s].astype(F32)
        sum_ref[pl.ds(pl.multiple_of(s * ROWS, ROWS), ROWS), :] = acc
        return carry

    lax.fori_loop(0, LIVE2, add, 0, unroll=4)
    slot = lax.broadcasted_iota(jnp.int32, (8, LANES), 0)
    accs = [jnp.zeros((8, LANES), F32) for _ in range(nhist + 1)]
    for jj in range(2):
        count = count_live(ti_ref, first, second + jj, capt, across * across)
        start = 0 if jj == 0 else (LIVE2 - count) * ROWS
        for g in range(capt // 8):
            alive = slot + g * 8 < count
            rows = slice(g * 8, (g + 1) * 8)

            def chunk(p, accs):
                here = pl.ds(pl.multiple_of(p * LANES, LANES), LANES)
                cycle = sum_ref[pl.ds(start + g * 8 * ROWS + p, 8, stride=ROWS), :]
                resid = jnp.where(alive, ovov_ref[0, jj, rows, here].astype(F32) + cycle, 0.0)
                moved = amps_ref[0, jj, rows, here].astype(F32) + resid * inv_ref[jj, rows, here]
                new_ref[0, jj, rows, here] = jnp.where(alive, moved, 0.0).astype(BF16)
                out = [
                    accs[m] + hist_ref[m, 0, jj, rows, here].astype(F32) * resid
                    for m in range(nhist)
                ]
                out.append(accs[nhist] + resid * resid)
                return out

            accs = lax.fori_loop(0, ROWS, chunk, accs, unroll=8)
    for m in range(8):
        if m <= nhist:
            gram_ref[m : m + 1] = jnp.sum(accs[m], axis=0, keepdims=True)
        else:
            gram_ref[m : m + 1] = jnp.zeros((1, LANES), F32)


def update(ti, amps, ovov, history, inv, parts, capt, across):
    nq = len(parts)
    return pl.pallas_call(
        functools.partial(update_kernel, capt, across, nq),
        in_specs=[SMEM] + [VMEM] * (4 + nq),
        out_specs=[VMEM, VMEM],
        out_shape=[
            jax.ShapeDtypeStruct(amps.shape, BF16),
            jax.ShapeDtypeStruct((8, LANES), F32),
        ],
        scratch_shapes=[pltpu.VMEM(((LIVE2 + capt) * ROWS, LANES), F32)],
        compiler_params=pltpu.CompilerParams(vmem_limit_bytes=24 * 1024 * 1024),
        cost_estimate=pl.CostEstimate(flops=10**8, bytes_accessed=6 * 10**6, transcendentals=0),
        name="update_amps",
    )(ti, amps, ovov, history, inv, *parts)


def finish_kernel(nhist, scale, *refs):
    total = refs[0][...]
    for ref in refs[1:-1]:
        total = total + ref[...]
    total = jnp.sum(total, axis=1, keepdims=True)
    row = lax.broadcasted_iota(jnp.int32, total.shape, 0)
    total = jnp.where(row == nhist, jnp.sqrt(jnp.maximum(total, 0.0)), total) * scale
    for m in range(nhist + 1):
        refs[-1][m] = total[m, 0]


def finish(sums, nhist, scale):
    return pl.pallas_call(
        functools.partial(finish_kernel, nhist, scale),
        in_specs=[VMEM] * len(sums),
        out_specs=SMEM,
        out_shape=jax.ShapeDtypeStruct((nhist + 1,), F32),
        name="finish_gram",
    )(*sums)


def swap(x, axis, size, step):
    return lax.ppermute(x, axis, [(n, n ^ step) for n in range(size)])


def spread_perm(npair, nq, m):
    pairs = []
    for plane in range(nq):
        for pair in range(npair):
            to = ((pair // 2) ^ m) * npair + 2 * plane + pair % 2
            pairs.append((plane * npair + pair, to))
    return pairs


def local(npair, nq, amps, tile_index, ovov, cycle_ints, history, slab, eps_occ, eps_vir):
    occ_dev, jdev, capt, tile_area = amps.shape
    ns = tile_index.shape[0]
    across = cycle_ints.shape[2]
    nhist = history.shape[0]
    assert occ_dev == 1 and jdev == 2 and tile_area == TILE * TILE and capt == 16
    assert ns == npair == 2 * nq
    packed = pack(amps, tile_index, capt, across)
    turned = [
        lax.ppermute(packed, ("reorder", "pair"), spread_perm(npair, nq, m)) for m in range(nq)
    ]
    late = lax.optimization_barrier((packed, cycle_ints, tile_index, slab, eps_occ, eps_vir))
    meta, mine, send, inv = prep(*late[1:], capt, across, nq)
    turned, send = lax.optimization_barrier((turned, send))
    theirs = swap(send, "pair", npair, 1)
    sums = multiply(0, meta, mine, turned, [], nq)
    partial = multiply(1, meta, theirs, turned, [sums], nq)
    parts = [partial[0]] + [swap(partial[e], "pair", npair, 2 * e) for e in range(1, nq)]
    new_amps, gram = update(tile_index, amps, ovov, history, inv, parts, capt, across)
    gram = sum([swap(gram, "pair", npair, n) for n in range(1, npair)], gram)
    sums = [gram] + [swap(gram, "reorder", nq, n) for n in range(1, nq)]
    return (new_amps, finish(sums, nhist, 1.0 / (TILE * ns)))


def solution(mesh):
    in_specs = (
        P("pair", "reorder", None, None),
        P(),
        P("pair", "reorder", None, None),
        P("pair", "reorder", None, None, None),
        P(None, "pair", "reorder", None, None),
        P(),
        P(),
        P(),
    )
    out_specs = (P("pair", "reorder", None, None), P())
    body = functools.partial(local, mesh.shape["pair"], mesh.shape["reorder"])
    return jax.shard_map(body, mesh=mesh, in_specs=in_specs, out_specs=out_specs, check_vma=False)
```

```python
import functools

import jax
import jax.numpy as jnp
from jax import lax
from jax.experimental import pallas as pl
from jax.experimental.pallas import tpu as pltpu
from jax.sharding import PartitionSpec as P

TILE = 64
ROWS = 32
LANES = 128
LIVE2 = 24
F32 = jnp.float32
BF16 = jnp.bfloat16
SMEM = pl.BlockSpec(memory_space=pltpu.SMEM)
VMEM = pl.BlockSpec(memory_space=pltpu.VMEM)


def count_live(ti_ref, i, j, capt, dead):
    total = jnp.int32(0)
    for s in range(capt):
        total = total + (ti_ref[i, j, s] < dead).astype(jnp.int32)
    return total


def row_of(idx, across):
    factor = -(-(1 << 17) // across)
    assert all((n * factor) >> 17 == n // across for n in range(across * across + 1))
    return lax.shift_right_logical(idx * factor, 17)


def pack_kernel(capt, across, ti_ref, amps_ref, out_ref, flat_ref, turned_ref):
    first = lax.axis_index("pair")
    second = lax.axis_index("reorder") * 2
    live1 = count_live(ti_ref, first, second + 1, capt, across * across)
    for jj in range(2):
        for p in range(ROWS):
            chunk = amps_ref[0, jj, :, p * LANES : (p + 1) * LANES].astype(F32)
            for g in range(capt // 8):
                start = (jj * capt + g * 8) * ROWS + p
                flat_ref[pl.ds(start, 8, stride=ROWS), :] = chunk[g * 8 : (g + 1) * 8]
    old = lax.broadcasted_iota(jnp.int32, (LANES, LANES), 0)
    new = lax.broadcasted_iota(jnp.int32, (LANES, LANES), 1)
    source = (new // 64) * 64 + (new % 32) * 2 + (new % 64) // 32
    turn = (old == source).astype(F32).astype(BF16)
    turned_ref[...] = jnp.dot(
        flat_ref[...].astype(BF16), turn, preferred_element_type=F32
    ).astype(BF16)
    out_ref[0:capt] = turned_ref[0 : capt * ROWS].reshape(capt, ROWS, LANES)
    out_ref[capt:LIVE2] = jnp.zeros((LIVE2 - capt, ROWS, LANES), BF16)

    def place(s, carry):
        start = pl.multiple_of((capt + s) * ROWS, ROWS)
        out_ref[LIVE2 - live1 + s] = turned_ref[pl.ds(start, ROWS), :]
        return carry

    lax.fori_loop(0, live1, place, 0)


def pack(amps, ti, capt, across):
    return pl.pallas_call(
        functools.partial(pack_kernel, capt, across),
        in_specs=[SMEM, VMEM],
        out_specs=VMEM,
        scratch_shapes=[
            pltpu.VMEM((2 * capt * ROWS, LANES), F32),
            pltpu.VMEM((2 * capt * ROWS, LANES), BF16),
        ],
        out_shape=jax.ShapeDtypeStruct((LIVE2, ROWS, LANES), BF16),
        cost_estimate=pl.CostEstimate(flops=10**8, bytes_accessed=500000, transcendentals=0),
        name="pack_amps",
    )(ti, amps)


def prep_kernel(
    capt, across, nq, nmax, ti_ref, hbm_ref,
    meta_ref, mine_ref, send_ref, ints_ref, wide_ref, tab_ref, sem,
):
    fetch_ints = pltpu.make_async_copy(hbm_ref, ints_ref, sem)
    fetch_ints.start()
    dead = across * across
    me = lax.axis_index("pair")
    sibling = me ^ 1
    plane = lax.axis_index("reorder")
    second = plane * 2

    def build(which, who, k):
        def field(f):
            return (which * 5 + f) * nmax

        parity = lax.rem(k, 2)

        def one_first(q, cnt):
            i = who ^ (q * 2)
            out = q * LIVE2
            for a in range(across + 1):
                tab_ref[a] = -1
            live_in = jnp.int32(0)
            for t in range(capt):
                idx = ti_ref[i, k, t]
                live_in = live_in + (idx < dead).astype(jnp.int32)
                a = row_of(idx, across)
                held = t * 32 + idx - a * across
                old = tab_ref[a]
                tab_ref[a] = jnp.where(old < 0, held, old)
                tab_ref[32 + a] = jnp.where(old < 0, -1, held)
            shift = q * LIVE2 + jnp.where(parity == 1, LIVE2 - live_in, 0)
            live1 = count_live(ti_ref, i, second + 1, capt, dead)
            for jj in range(2):
                for s in range(capt):
                    idx = ti_ref[i, second + jj, s]
                    a = row_of(idx, across)
                    b = idx - a * across
                    h0 = tab_ref[a]
                    h1 = tab_ref[32 + a]
                    hit = (idx < dead) & (h0 >= 0)
                    both = h1 >= 0
                    if which < 2:
                        place = out + (s if jj == 0 else LIVE2 - live1 + s)
                        meta_ref[field(0) + cnt] = place
                        t0 = shift + lax.shift_right_arithmetic(h0, 5)
                        t1 = shift + lax.shift_right_arithmetic(h1, 5)
                        meta_ref[field(1) + cnt] = t0
                        meta_ref[field(2) + cnt] = jnp.where(both, t1, t0)
                    if which != 1:
                        w0 = ((h0 & 31) * across + b) * 2 + jj
                        w1 = ((h1 & 31) * across + b) * 2 + jj
                        meta_ref[field(3) + cnt] = w0
                        meta_ref[field(4) + cnt] = jnp.where(both, w1, -1)
                    cnt = cnt + hit.astype(jnp.int32)
            return cnt

        total = lax.fori_loop(0, nq, one_first, jnp.int32(0))
        meta_ref[15 * nmax + which] = total
        return total

    def gather(which, total, tiles_ref):
        def fetch(step, carry):
            for u in range(4):
                e = jnp.minimum(step * 4 + u, total - 1)
                for m in range(2):
                    at = jnp.maximum(meta_ref[(which * 5 + 3 + m) * nmax + e], 0)
                    wide_ref[2 * u + m] = ints_ref[lax.shift_right_logical(at, 1)].astype(F32)
            for u in range(4):
                e = jnp.minimum(step * 4 + u, total - 1)
                for m in range(2):
                    at = meta_ref[(which * 5 + 3 + m) * nmax + e]
                    jj = jnp.maximum(at, 0) & 1
                    tile = wide_ref[2 * u + m, pl.ds(jj, ROWS, stride=2), :]
                    if m == 1:
                        tile = jnp.where(at >= 0, tile, 0.0)
                    tiles_ref[e, m * ROWS : (m + 1) * ROWS] = tile.astype(BF16)
            return carry

        lax.fori_loop(0, (total + 3) // 4, fetch, 0)

    total_send = build(2, sibling, me)
    total_mine = build(0, me, me)
    build(1, me, sibling)
    fetch_ints.wait()
    gather(2, total_send, send_ref)
    gather(0, total_mine, mine_ref)


def prep(cycle_ints, ti, capt, across, nq):
    nmax = nq * LIVE2 + 8
    ints = cycle_ints[0].transpose(1, 2, 0, 3).reshape(across, across, 2, ROWS, LANES)
    ints = ints.transpose(0, 1, 3, 2, 4).reshape(across * across, 2 * ROWS, LANES)
    tiles = jax.ShapeDtypeStruct((nq * LIVE2, 2 * ROWS, LANES), BF16)
    return pl.pallas_call(
        functools.partial(prep_kernel, capt, across, nq, nmax),
        in_specs=[SMEM, pl.BlockSpec(memory_space=pltpu.HBM)],
        out_specs=[SMEM, VMEM, VMEM],
        scratch_shapes=[
            pltpu.VMEM(ints.shape, BF16),
            pltpu.VMEM((8, 2 * ROWS, LANES), F32),
            pltpu.SMEM((64,), jnp.int32),
            pltpu.SemaphoreType.DMA,
        ],
        out_shape=[jax.ShapeDtypeStruct((15 * nmax + 8,), jnp.int32), tiles, tiles],
        compiler_params=pltpu.CompilerParams(vmem_limit_bytes=53 * 1024 * 1024),
        cost_estimate=pl.CostEstimate(flops=10**9, bytes_accessed=40 * 10**6, transcendentals=0),
        name="prep_integrals",
    )(ti, ints)


def denom_kernel(capt, across, ti_ref, slab_ref, occ_ref, vir_ref, inv_ref, row_ref, col_ref):
    first = lax.axis_index("pair")
    second = lax.axis_index("reorder") * 2
    occ_i = occ_ref[slab_ref[first]]
    low = lax.broadcasted_iota(jnp.int32, (8, LANES), 1) < 64
    for jj in range(2):
        for s in range(capt):
            idx = ti_ref[first, second + jj, s]
            row = row_of(idx, across)
            a = jnp.minimum(row, across - 1)
            b = idx - row * across
            row_ref[jj * capt + s] = vir_ref[a]
            col_ref[jj * capt + s] = vir_ref[b]
    for jj in range(2):
        occ = occ_i + occ_ref[slab_ref[second + jj]]
        for g in range(capt // 8):
            here = pl.ds(jj * capt + g * 8, 8)
            rows = occ - row_ref[here]
            col = col_ref[here]
            cols = jnp.concatenate([col, col], axis=1)
            for p in range(ROWS):
                even = jnp.broadcast_to(rows[:, 2 * p : 2 * p + 1], (8, LANES))
                odd = jnp.broadcast_to(rows[:, 2 * p + 1 : 2 * p + 2], (8, LANES))
                inv_ref[jj, g * 8 : (g + 1) * 8, p * LANES : (p + 1) * LANES] = 1.0 / (
                    jnp.where(low, even, odd) - cols
                )


def denominators(ti, slab, eps_occ, eps_vir, capt, across):
    return pl.pallas_call(
        functools.partial(denom_kernel, capt, across),
        in_specs=[SMEM, SMEM, SMEM, VMEM],
        out_specs=VMEM,
        scratch_shapes=[pltpu.VMEM((2 * capt, 64), F32)] * 2,
        out_shape=jax.ShapeDtypeStruct((2, capt, TILE * TILE), F32),
        cost_estimate=pl.CostEstimate(flops=10**7, bytes_accessed=10**6, transcendentals=0),
        name="denominators",
    )(ti, slab, eps_occ, eps_vir.reshape(across, 64))


def multiply_kernel(which, nq, nmax, unroll, meta_ref, tiles_ref, *refs):
    amps_refs, refs = refs[:nq], refs[nq:]
    if which == 0:
        sum_ref, amps_ref = refs
        sum_ref[...] = jnp.zeros(sum_ref.shape, F32)
    else:
        sum_ref, out_refs, amps_ref = refs[0], refs[1:-1], refs[-1]
    for q in range(nq):
        amps_ref[q * LIVE2 : (q + 1) * LIVE2] = amps_refs[q][...]
    low = lax.broadcasted_iota(jnp.int32, (ROWS, LANES), 1) < 64

    def spread(w):
        w = w.astype(F32)
        r = pltpu.roll(w, 64, 1)
        zero = jnp.zeros_like(w)
        parts = [
            jnp.where(low, w, zero),
            jnp.where(low, r, zero),
            jnp.where(low, zero, r),
            jnp.where(low, zero, w),
        ]
        return jnp.concatenate(parts, axis=0).astype(BF16)

    total = meta_ref[15 * nmax + which]

    def several(step, carry):
        results = []
        for u in range(unroll):
            e = jnp.minimum(step * unroll + u, total - 1)
            at = which * 5 * nmax + e
            left = jnp.concatenate(
                [amps_ref[meta_ref[nmax + at]], amps_ref[meta_ref[2 * nmax + at]]], axis=1
            )
            right = jnp.concatenate(
                [spread(tiles_ref[e, 0:ROWS]), spread(tiles_ref[e, ROWS : 2 * ROWS])], axis=0
            )
            place = jnp.where(step * unroll + u < total, meta_ref[at], nq * LIVE2)
            results.append((place, jnp.dot(left, right, preferred_element_type=F32)))
        for place, value in results:
            if which == 0:
                sum_ref[place] = value
            else:
                sum_ref[place] += value
        return carry

    lax.fori_loop(0, (total + unroll - 1) // unroll, several, 0)
    if which == 1:
        for q in range(nq):
            out_refs[q][...] = sum_ref[q * LIVE2 : (q + 1) * LIVE2].astype(BF16)


def multiply(which, meta, tiles, amps, sums, nq):
    block = jax.ShapeDtypeStruct((LIVE2, ROWS, LANES), BF16)
    scratch = [pltpu.VMEM((nq * LIVE2, ROWS, LANES), BF16)]
    if which == 0:
        out = jax.ShapeDtypeStruct((nq * LIVE2 + 1, ROWS, LANES), F32)
    else:
        out = [block] * nq
    return pl.pallas_call(
        functools.partial(multiply_kernel, which, nq, nq * LIVE2 + 8, 8),
        in_specs=[SMEM] + [VMEM] * (1 + nq + len(sums)),
        out_specs=jax.tree.map(lambda _: VMEM, out),
        out_shape=out,
        scratch_shapes=scratch,
        compiler_params=pltpu.CompilerParams(vmem_limit_bytes=24 * 1024 * 1024),
        cost_estimate=pl.CostEstimate(flops=10**9, bytes_accessed=10**7, transcendentals=0),
        name="multiply_own" if which == 0 else "multiply_sibling",
    )(meta, tiles, *amps, *sums)


def update_kernel(
    capt, across, nq, ti_ref, amps_ref, ovov_ref, hist_ref, inv_ref, *refs
):
    part_refs, (new_ref, gram_ref, sum_ref) = refs[:nq], refs[nq:]
    nhist = hist_ref.shape[0]
    first = lax.axis_index("pair")
    second = lax.axis_index("reorder") * 2

    def add(s, carry):
        acc = part_refs[0][s].astype(F32)
        for part_ref in part_refs[1:]:
            acc = acc + part_ref[s].astype(F32)
        sum_ref[pl.ds(pl.multiple_of(s * ROWS, ROWS), ROWS), :] = acc
        return carry

    lax.fori_loop(0, LIVE2, add, 0, unroll=4)
    slot = lax.broadcasted_iota(jnp.int32, (8, LANES), 0)
    accs = [jnp.zeros((8, LANES), F32) for _ in range(nhist + 1)]
    for jj in range(2):
        count = count_live(ti_ref, first, second + jj, capt, across * across)
        start = 0 if jj == 0 else (LIVE2 - count) * ROWS
        for g in range(capt // 8):
            alive = slot + g * 8 < count
            rows = slice(g * 8, (g + 1) * 8)

            def chunk(p, accs):
                here = pl.ds(pl.multiple_of(p * LANES, LANES), LANES)
                cycle = sum_ref[pl.ds(start + g * 8 * ROWS + p, 8, stride=ROWS), :]
                resid = jnp.where(alive, ovov_ref[0, jj, rows, here].astype(F32) + cycle, 0.0)
                moved = amps_ref[0, jj, rows, here].astype(F32) + resid * inv_ref[jj, rows, here]
                new_ref[0, jj, rows, here] = jnp.where(alive, moved, 0.0).astype(BF16)
                out = [
                    accs[m] + hist_ref[m, 0, jj, rows, here].astype(F32) * resid
                    for m in range(nhist)
                ]
                out.append(accs[nhist] + resid * resid)
                return out

            accs = lax.fori_loop(0, ROWS, chunk, accs, unroll=8)
    for m in range(8):
        row = jnp.zeros((1, LANES), F32)
        if m <= nhist:
            row = jnp.sum(accs[m], axis=0, keepdims=True)
        for n in range(gram_ref.shape[0]):
            gram_ref[n, m : m + 1] = row


def update(ti, amps, ovov, history, inv, parts, copies, capt, across):
    nq = len(parts)
    return pl.pallas_call(
        functools.partial(update_kernel, capt, across, nq),
        in_specs=[SMEM] + [VMEM] * (4 + nq),
        out_specs=[VMEM, VMEM],
        out_shape=[
            jax.ShapeDtypeStruct(amps.shape, BF16),
            jax.ShapeDtypeStruct((copies, 8, LANES), F32),
        ],
        scratch_shapes=[pltpu.VMEM(((LIVE2 + capt) * ROWS, LANES), F32)],
        compiler_params=pltpu.CompilerParams(vmem_limit_bytes=24 * 1024 * 1024),
        cost_estimate=pl.CostEstimate(flops=10**8, bytes_accessed=6 * 10**6, transcendentals=0),
        name="update_amps",
    )(ti, amps, ovov, history, inv, *parts)


def finish_kernel(nhist, scale, *refs):
    total = jnp.sum(refs[0][...], axis=0)
    total = jnp.sum(total, axis=1, keepdims=True)
    row = lax.broadcasted_iota(jnp.int32, total.shape, 0)
    total = jnp.where(row == nhist, jnp.sqrt(jnp.maximum(total, 0.0)), total) * scale
    for m in range(nhist + 1):
        refs[-1][m] = total[m, 0]


def finish(sums, nhist, scale):
    return pl.pallas_call(
        functools.partial(finish_kernel, nhist, scale),
        in_specs=[VMEM],
        out_specs=SMEM,
        out_shape=jax.ShapeDtypeStruct((nhist + 1,), F32),
        name="finish_gram",
    )(sums)


def swap(x, axis, size, step):
    return lax.ppermute(x, axis, [(n, n ^ step) for n in range(size)])


def local(npair, nq, amps, tile_index, ovov, cycle_ints, history, slab, eps_occ, eps_vir):
    occ_dev, jdev, capt, tile_area = amps.shape
    ns = tile_index.shape[0]
    across = cycle_ints.shape[2]
    nhist = history.shape[0]
    assert occ_dev == 1 and jdev == 2 and tile_area == TILE * TILE and capt == 16
    assert ns == npair == 2 * nq
    packed = pack(amps, tile_index, capt, across)
    blocks = lax.all_gather(packed, "reorder")
    late = lax.optimization_barrier((blocks, cycle_ints, tile_index))
    meta, mine, send = prep(*late[1:], capt, across, nq)
    chip = lax.axis_index("pair") // 2
    turned = [
        lax.dynamic_index_in_dim(blocks, chip ^ e, 0, keepdims=False) for e in range(nq)
    ]
    turned = [turned[0]] + [swap(turned[e], "pair", npair, 2 * e) for e in range(1, nq)]
    turned, send = lax.optimization_barrier((turned, send))
    theirs = swap(send, "pair", npair, 1)
    sums = multiply(0, meta, mine, turned, [], nq)
    partial = multiply(1, meta, theirs, turned, [sums], nq)
    parts = [partial[0]] + [swap(partial[e], "pair", npair, 2 * e) for e in range(1, nq)]
    late = lax.optimization_barrier((partial[0], tile_index, slab, eps_occ, eps_vir))
    inv = denominators(*late[1:], capt, across)
    new_amps, gram = update(
        tile_index, amps, ovov, history, inv, parts, npair, capt, across
    )
    gram = lax.all_to_all(gram, "pair", split_axis=0, concat_axis=0, tiled=True)
    sums = lax.all_gather(jnp.sum(gram, axis=0), "reorder")
    return (new_amps, finish(sums, nhist, 1.0 / (TILE * ns)))


def solution(mesh):
    in_specs = (
        P("pair", "reorder", None, None),
        P(),
        P("pair", "reorder", None, None),
        P("pair", "reorder", None, None, None),
        P(None, "pair", "reorder", None, None),
        P(),
        P(),
        P(),
    )
    out_specs = (P("pair", "reorder", None, None), P())
    body = functools.partial(local, mesh.shape["pair"], mesh.shape["reorder"])
    return jax.shard_map(body, mesh=mesh, in_specs=in_specs, out_specs=out_specs, check_vma=False)
```

```python
import functools

import jax
import jax.numpy as jnp
from jax import lax
from jax.experimental import pallas as pl
from jax.experimental.pallas import tpu as pltpu
from jax.sharding import PartitionSpec as P

TILE = 64
ROWS = 32
LANES = 128
LIVE2 = 24
F32 = jnp.float32
BF16 = jnp.bfloat16
SMEM = pl.BlockSpec(memory_space=pltpu.SMEM)
VMEM = pl.BlockSpec(memory_space=pltpu.VMEM)


def count_live(ti_ref, i, j, capt, dead):
    total = jnp.int32(0)
    for s in range(capt):
        total = total + (ti_ref[i, j, s] < dead).astype(jnp.int32)
    return total


def row_of(idx, across):
    factor = -(-(1 << 17) // across)
    assert all((n * factor) >> 17 == n // across for n in range(across * across + 1))
    return lax.shift_right_logical(idx * factor, 17)


def pack_kernel(capt, across, ti_ref, amps_ref, out_ref, flat_ref, turned_ref):
    first = lax.axis_index("pair")
    second = lax.axis_index("reorder") * 2
    live1 = count_live(ti_ref, first, second + 1, capt, across * across)
    for jj in range(2):
        for p in range(ROWS):
            chunk = amps_ref[0, jj, :, p * LANES : (p + 1) * LANES].astype(F32)
            for g in range(capt // 8):
                start = (jj * capt + g * 8) * ROWS + p
                flat_ref[pl.ds(start, 8, stride=ROWS), :] = chunk[g * 8 : (g + 1) * 8]
    old = lax.broadcasted_iota(jnp.int32, (LANES, LANES), 0)
    new = lax.broadcasted_iota(jnp.int32, (LANES, LANES), 1)
    source = (new // 64) * 64 + (new % 32) * 2 + (new % 64) // 32
    turn = (old == source).astype(F32).astype(BF16)
    turned_ref[...] = jnp.dot(
        flat_ref[...].astype(BF16), turn, preferred_element_type=F32
    ).astype(BF16)
    out_ref[0:capt] = turned_ref[0 : capt * ROWS].reshape(capt, ROWS, LANES)
    out_ref[capt:LIVE2] = jnp.zeros((LIVE2 - capt, ROWS, LANES), BF16)

    def place(s, carry):
        start = pl.multiple_of((capt + s) * ROWS, ROWS)
        out_ref[LIVE2 - live1 + s] = turned_ref[pl.ds(start, ROWS), :]
        return carry

    lax.fori_loop(0, live1, place, 0)


def pack(amps, ti, capt, across):
    return pl.pallas_call(
        functools.partial(pack_kernel, capt, across),
        in_specs=[SMEM, VMEM],
        out_specs=VMEM,
        scratch_shapes=[
            pltpu.VMEM((2 * capt * ROWS, LANES), F32),
            pltpu.VMEM((2 * capt * ROWS, LANES), BF16),
        ],
        out_shape=jax.ShapeDtypeStruct((LIVE2, ROWS, LANES), BF16),
        cost_estimate=pl.CostEstimate(flops=10**8, bytes_accessed=500000, transcendentals=0),
        name="pack_amps",
    )(ti, amps)


def prep_kernel(
    capt, across, nq, nmax, ti_ref, hbm_ref,
    meta_ref, mine_ref, send_ref, ints_ref, wide_ref, tab_ref, sem,
):
    fetch_ints = pltpu.make_async_copy(hbm_ref, ints_ref, sem)
    fetch_ints.start()
    dead = across * across
    me = lax.axis_index("pair")
    sibling = me ^ 1
    plane = lax.axis_index("reorder")
    second = plane * 2

    def build(which, who, k):
        def field(f):
            return (which * 5 + f) * nmax

        parity = lax.rem(k, 2)

        def one_first(q, cnt):
            i = (plane ^ q) * 2 + (who & 1)
            out = (lax.shift_right_logical(who, 1) ^ plane ^ q) * LIVE2
            for a in range(across + 1):
                tab_ref[a] = -1
            live_in = jnp.int32(0)
            for t in range(capt):
                idx = ti_ref[i, k, t]
                live_in = live_in + (idx < dead).astype(jnp.int32)
                a = row_of(idx, across)
                held = t * 32 + idx - a * across
                old = tab_ref[a]
                tab_ref[a] = jnp.where(old < 0, held, old)
                tab_ref[32 + a] = jnp.where(old < 0, -1, held)
            shift = q * LIVE2 + jnp.where(parity == 1, LIVE2 - live_in, 0)
            live1 = count_live(ti_ref, i, second + 1, capt, dead)
            for jj in range(2):
                for s in range(capt):
                    idx = ti_ref[i, second + jj, s]
                    a = row_of(idx, across)
                    b = idx - a * across
                    h0 = tab_ref[a]
                    h1 = tab_ref[32 + a]
                    hit = (idx < dead) & (h0 >= 0)
                    both = h1 >= 0
                    if which < 2:
                        place = out + (s if jj == 0 else LIVE2 - live1 + s)
                        meta_ref[field(0) + cnt] = place
                        t0 = shift + lax.shift_right_arithmetic(h0, 5)
                        t1 = shift + lax.shift_right_arithmetic(h1, 5)
                        meta_ref[field(1) + cnt] = t0
                        meta_ref[field(2) + cnt] = jnp.where(both, t1, t0)
                    if which != 1:
                        w0 = ((h0 & 31) * across + b) * 2 + jj
                        w1 = ((h1 & 31) * across + b) * 2 + jj
                        meta_ref[field(3) + cnt] = w0
                        meta_ref[field(4) + cnt] = jnp.where(both, w1, -1)
                    cnt = cnt + hit.astype(jnp.int32)
            return cnt

        total = lax.fori_loop(0, nq, one_first, jnp.int32(0))
        meta_ref[15 * nmax + which] = total
        return total

    def gather(which, total, tiles_ref):
        def fetch(step, carry):
            for u in range(4):
                e = jnp.minimum(step * 4 + u, total - 1)
                for m in range(2):
                    at = jnp.maximum(meta_ref[(which * 5 + 3 + m) * nmax + e], 0)
                    wide_ref[2 * u + m] = ints_ref[lax.shift_right_logical(at, 1)].astype(F32)
            for u in range(4):
                e = jnp.minimum(step * 4 + u, total - 1)
                for m in range(2):
                    at = meta_ref[(which * 5 + 3 + m) * nmax + e]
                    jj = jnp.maximum(at, 0) & 1
                    tile = wide_ref[2 * u + m, pl.ds(jj, ROWS, stride=2), :]
                    if m == 1:
                        tile = jnp.where(at >= 0, tile, 0.0)
                    tiles_ref[e, m * ROWS : (m + 1) * ROWS] = tile.astype(BF16)
            return carry

        lax.fori_loop(0, (total + 3) // 4, fetch, 0)

    total_send = build(2, sibling, me)
    total_mine = build(0, me, me)
    build(1, me, sibling)
    fetch_ints.wait()
    gather(2, total_send, send_ref)
    gather(0, total_mine, mine_ref)


def prep(cycle_ints, ti, capt, across, nq):
    nmax = nq * LIVE2 + 8
    ints = cycle_ints[0].transpose(1, 2, 0, 3).reshape(across, across, 2, ROWS, LANES)
    ints = ints.transpose(0, 1, 3, 2, 4).reshape(across * across, 2 * ROWS, LANES)
    tiles = jax.ShapeDtypeStruct((nq * LIVE2, 2 * ROWS, LANES), BF16)
    return pl.pallas_call(
        functools.partial(prep_kernel, capt, across, nq, nmax),
        in_specs=[SMEM, pl.BlockSpec(memory_space=pltpu.HBM)],
        out_specs=[SMEM, VMEM, VMEM],
        scratch_shapes=[
            pltpu.VMEM(ints.shape, BF16),
            pltpu.VMEM((8, 2 * ROWS, LANES), F32),
            pltpu.SMEM((64,), jnp.int32),
            pltpu.SemaphoreType.DMA,
        ],
        out_shape=[jax.ShapeDtypeStruct((15 * nmax + 8,), jnp.int32), tiles, tiles],
        compiler_params=pltpu.CompilerParams(vmem_limit_bytes=53 * 1024 * 1024),
        cost_estimate=pl.CostEstimate(flops=10**9, bytes_accessed=40 * 10**6, transcendentals=0),
        name="prep_integrals",
    )(ti, ints)


def denom_kernel(capt, across, ti_ref, slab_ref, occ_ref, vir_ref, inv_ref, row_ref, col_ref):
    first = lax.axis_index("pair")
    second = lax.axis_index("reorder") * 2
    occ_i = occ_ref[slab_ref[first]]
    low = lax.broadcasted_iota(jnp.int32, (8, LANES), 1) < 64
    for jj in range(2):
        for s in range(capt):
            idx = ti_ref[first, second + jj, s]
            row = row_of(idx, across)
            a = jnp.minimum(row, across - 1)
            b = idx - row * across
            row_ref[jj * capt + s] = vir_ref[a]
            col_ref[jj * capt + s] = vir_ref[b]
    for jj in range(2):
        occ = occ_i + occ_ref[slab_ref[second + jj]]
        for g in range(capt // 8):
            here = pl.ds(jj * capt + g * 8, 8)
            rows = occ - row_ref[here]
            col = col_ref[here]
            cols = jnp.concatenate([col, col], axis=1)
            for p in range(ROWS):
                even = jnp.broadcast_to(rows[:, 2 * p : 2 * p + 1], (8, LANES))
                odd = jnp.broadcast_to(rows[:, 2 * p + 1 : 2 * p + 2], (8, LANES))
                inv_ref[jj, g * 8 : (g + 1) * 8, p * LANES : (p + 1) * LANES] = 1.0 / (
                    jnp.where(low, even, odd) - cols
                )


def denominators(ti, slab, eps_occ, eps_vir, capt, across):
    return pl.pallas_call(
        functools.partial(denom_kernel, capt, across),
        in_specs=[SMEM, SMEM, SMEM, VMEM],
        out_specs=VMEM,
        scratch_shapes=[pltpu.VMEM((2 * capt, 64), F32)] * 2,
        out_shape=jax.ShapeDtypeStruct((2, capt, TILE * TILE), F32),
        cost_estimate=pl.CostEstimate(flops=10**7, bytes_accessed=10**6, transcendentals=0),
        name="denominators",
    )(ti, slab, eps_occ, eps_vir.reshape(across, 64))


def multiply_kernel(which, nq, nmax, unroll, meta_ref, tiles_ref, *refs):
    amps_refs, refs = refs[:nq], refs[nq:]
    if which == 0:
        sum_ref, amps_ref = refs
        sum_ref[...] = jnp.zeros(sum_ref.shape, F32)
    else:
        sum_ref, out_refs, amps_ref = refs[0], refs[1:-1], refs[-1]
    for q in range(nq):
        amps_ref[q * LIVE2 : (q + 1) * LIVE2] = amps_refs[q][...]
    low = lax.broadcasted_iota(jnp.int32, (ROWS, LANES), 1) < 64

    def spread(w):
        w = w.astype(F32)
        r = pltpu.roll(w, 64, 1)
        zero = jnp.zeros_like(w)
        parts = [
            jnp.where(low, w, zero),
            jnp.where(low, r, zero),
            jnp.where(low, zero, r),
            jnp.where(low, zero, w),
        ]
        return jnp.concatenate(parts, axis=0).astype(BF16)

    total = meta_ref[15 * nmax + which]

    def several(step, carry):
        results = []
        for u in range(unroll):
            e = jnp.minimum(step * unroll + u, total - 1)
            at = which * 5 * nmax + e
            left = jnp.concatenate(
                [amps_ref[meta_ref[nmax + at]], amps_ref[meta_ref[2 * nmax + at]]], axis=1
            )
            right = jnp.concatenate(
                [spread(tiles_ref[e, 0:ROWS]), spread(tiles_ref[e, ROWS : 2 * ROWS])], axis=0
            )
            place = jnp.where(step * unroll + u < total, meta_ref[at], nq * LIVE2)
            results.append((place, jnp.dot(left, right, preferred_element_type=F32)))
        for place, value in results:
            if which == 0:
                sum_ref[place] = value
            else:
                sum_ref[place] += value
        return carry

    lax.fori_loop(0, (total + unroll - 1) // unroll, several, 0)
    if which == 1:
        for q in range(nq):
            out_refs[q][...] = sum_ref[q * LIVE2 : (q + 1) * LIVE2].astype(BF16)


def multiply(which, meta, tiles, amps, sums, nq):
    block = jax.ShapeDtypeStruct((LIVE2, ROWS, LANES), BF16)
    total = jax.ShapeDtypeStruct((nq * LIVE2 + 1, ROWS, LANES), F32)
    out = [block] * nq if which == 1 else total
    return pl.pallas_call(
        functools.partial(multiply_kernel, which, nq, nq * LIVE2 + 8, 8),
        in_specs=[SMEM] + [VMEM] * (1 + len(amps) + len(sums)),
        out_specs=jax.tree.map(lambda _: VMEM, out),
        out_shape=out,
        scratch_shapes=[pltpu.VMEM((nq * LIVE2, ROWS, LANES), BF16)],
        compiler_params=pltpu.CompilerParams(vmem_limit_bytes=24 * 1024 * 1024),
        cost_estimate=pl.CostEstimate(flops=10**9, bytes_accessed=6 * 10**6, transcendentals=0),
        name=("multiply_own", "multiply_sibling")[which],
    )(meta, tiles, *amps, *sums)


def update_kernel(
    capt, across, nq, ti_ref, amps_ref, ovov_ref, hist_ref, inv_ref, *refs
):
    part_refs, (new_ref, gram_ref, sum_ref) = refs[:nq], refs[nq:]
    nhist = hist_ref.shape[0]
    first = lax.axis_index("pair")
    second = lax.axis_index("reorder") * 2

    def add(s, carry):
        acc = part_refs[0][s].astype(F32)
        for part_ref in part_refs[1:]:
            acc = acc + part_ref[s].astype(F32)
        sum_ref[pl.ds(pl.multiple_of(s * ROWS, ROWS), ROWS), :] = acc
        return carry

    lax.fori_loop(0, LIVE2, add, 0, unroll=4)
    slot = lax.broadcasted_iota(jnp.int32, (capt, LANES), 0)
    accs = [jnp.zeros((capt, LANES), F32) for _ in range(nhist + 1)]
    for jj in range(2):
        count = count_live(ti_ref, first, second + jj, capt, across * across)
        start = 0 if jj == 0 else (LIVE2 - count) * ROWS
        alive = slot < count

        def chunk(p, accs):
            here = pl.ds(pl.multiple_of(p * LANES, LANES), LANES)
            cycle = jnp.concatenate(
                [
                    sum_ref[pl.ds(start + g * ROWS + p, 8, stride=ROWS), :]
                    for g in range(0, capt, 8)
                ],
                axis=0,
            )
            resid = jnp.where(alive, ovov_ref[0, jj, :, here].astype(F32) + cycle, 0.0)
            moved = amps_ref[0, jj, :, here].astype(F32) + resid * inv_ref[jj, :, here]
            new_ref[0, jj, :, here] = jnp.where(alive, moved, 0.0).astype(BF16)
            out = [
                accs[m] + hist_ref[m, 0, jj, :, here].astype(F32) * resid for m in range(nhist)
            ]
            out.append(accs[nhist] + resid * resid)
            return out

        accs = lax.fori_loop(0, ROWS, chunk, accs, unroll=4)
    for m in range(8):
        row = jnp.zeros((1, LANES), F32)
        if m <= nhist:
            row = jnp.sum(accs[m], axis=0, keepdims=True)
        gram_ref[m : m + 1] = row


def update(ti, amps, ovov, history, inv, parts, capt, across):
    nq = len(parts)
    return pl.pallas_call(
        functools.partial(update_kernel, capt, across, nq),
        in_specs=[SMEM] + [VMEM] * (4 + nq),
        out_specs=[VMEM, VMEM],
        out_shape=[
            jax.ShapeDtypeStruct(amps.shape, BF16),
            jax.ShapeDtypeStruct((8, LANES), F32),
        ],
        scratch_shapes=[pltpu.VMEM(((LIVE2 + capt) * ROWS, LANES), F32)],
        compiler_params=pltpu.CompilerParams(vmem_limit_bytes=24 * 1024 * 1024),
        cost_estimate=pl.CostEstimate(flops=10**8, bytes_accessed=6 * 10**6, transcendentals=0),
        name="update_amps",
    )(ti, amps, ovov, history, inv, *parts)


def finish_kernel(nhist, scale, *refs):
    total = refs[0][...] + refs[1][...]
    total = jnp.sum(total, axis=1, keepdims=True)
    row = lax.broadcasted_iota(jnp.int32, total.shape, 0)
    total = jnp.where(row == nhist, jnp.sqrt(jnp.maximum(total, 0.0)), total) * scale
    for m in range(nhist + 1):
        refs[-1][m] = total[m, 0]


def finish(sums, nhist, scale):
    return pl.pallas_call(
        functools.partial(finish_kernel, nhist, scale),
        in_specs=[VMEM] * len(sums),
        out_specs=SMEM,
        out_shape=jax.ShapeDtypeStruct((nhist + 1,), F32),
        name="finish_gram",
    )(*sums)


def swap(x, axis, size, step):
    return lax.ppermute(x, axis, [(n, n ^ step) for n in range(size)])


def spread_perm(npair, nq, m):
    return [
        (z * npair + p, ((p // 2) ^ m) * npair + 2 * z + p % 2)
        for z in range(nq)
        for p in range(npair)
    ]


def local(npair, nq, amps, tile_index, ovov, cycle_ints, history, slab, eps_occ, eps_vir):
    occ_dev, jdev, capt, tile_area = amps.shape
    ns = tile_index.shape[0]
    across = cycle_ints.shape[2]
    nhist = history.shape[0]
    assert occ_dev == 1 and jdev == 2 and tile_area == TILE * TILE and capt == 16
    assert ns == npair == 2 * nq
    packed = pack(amps, tile_index, capt, across)
    axes = ("reorder", "pair")
    turned = [lax.ppermute(packed, axes, spread_perm(npair, nq, m)) for m in range(nq)]
    late = lax.optimization_barrier((packed, cycle_ints, tile_index, slab, eps_occ, eps_vir))
    meta, mine, send = prep(*late[1:3], capt, across, nq)
    inv = denominators(*late[2:], capt, across)
    turned, send, inv = lax.optimization_barrier((turned, send, inv))
    theirs = swap(send, "pair", npair, 1)
    sums = multiply(0, meta, mine, turned, [], nq)
    partial = multiply(1, meta, theirs, turned, [sums], nq)
    parts = [partial[0]] + [swap(partial[e], "pair", npair, 2 * e) for e in range(1, nq)]
    new_amps, gram = update(tile_index, amps, ovov, history, inv, parts, capt, across)
    step = 1
    while step < npair:
        gram = gram + swap(gram, "pair", npair, step)
        step *= 2
    step = 1
    while 2 * step < nq:
        gram = gram + swap(gram, "reorder", nq, step)
        step *= 2
    sums = [gram, swap(gram, "reorder", nq, step)]
    return (new_amps, finish(sums, nhist, 1.0 / (TILE * ns)))


def solution(mesh):
    in_specs = (
        P("pair", "reorder", None, None),
        P(),
        P("pair", "reorder", None, None),
        P("pair", "reorder", None, None, None),
        P(None, "pair", "reorder", None, None),
        P(),
        P(),
        P(),
    )
    out_specs = (P("pair", "reorder", None, None), P())
    body = functools.partial(local, mesh.shape["pair"], mesh.shape["reorder"])
    return jax.shard_map(body, mesh=mesh, in_specs=in_specs, out_specs=out_specs, check_vma=False)
```

```python
import functools

import jax
import jax.numpy as jnp
from jax import lax
from jax.experimental import pallas as pl
from jax.experimental.pallas import tpu as pltpu
from jax.sharding import PartitionSpec as P

TILE = 64
ROWS = 32
LANES = 128
LIVE2 = 24
F32 = jnp.float32
BF16 = jnp.bfloat16
SMEM = pl.BlockSpec(memory_space=pltpu.SMEM)
VMEM = pl.BlockSpec(memory_space=pltpu.VMEM)


def count_live(ti_ref, i, j, capt, dead):
    total = jnp.int32(0)
    for s in range(capt):
        total = total + (ti_ref[i, j, s] < dead).astype(jnp.int32)
    return total


def row_of(idx, across):
    factor = -(-(1 << 17) // across)
    assert all((n * factor) >> 17 == n // across for n in range(across * across + 1))
    return lax.shift_right_logical(idx * factor, 17)


def pack_kernel(capt, across, ti_ref, amps_ref, out_ref, flat_ref, turned_ref):
    first = lax.axis_index("pair")
    second = lax.axis_index("reorder") * 2
    live1 = count_live(ti_ref, first, second + 1, capt, across * across)
    for jj in range(2):
        for p in range(ROWS):
            chunk = amps_ref[0, jj, :, p * LANES : (p + 1) * LANES].astype(F32)
            for g in range(capt // 8):
                start = (jj * capt + g * 8) * ROWS + p
                flat_ref[pl.ds(start, 8, stride=ROWS), :] = chunk[g * 8 : (g + 1) * 8]
    old = lax.broadcasted_iota(jnp.int32, (LANES, LANES), 0)
    new = lax.broadcasted_iota(jnp.int32, (LANES, LANES), 1)
    source = (new // 64) * 64 + (new % 32) * 2 + (new % 64) // 32
    turn = (old == source).astype(F32).astype(BF16)
    turned_ref[...] = jnp.dot(
        flat_ref[...].astype(BF16), turn, preferred_element_type=F32
    ).astype(BF16)
    out_ref[0:capt] = turned_ref[0 : capt * ROWS].reshape(capt, ROWS, LANES)
    out_ref[capt:LIVE2] = jnp.zeros((LIVE2 - capt, ROWS, LANES), BF16)

    def place(s, carry):
        start = pl.multiple_of((capt + s) * ROWS, ROWS)
        out_ref[LIVE2 - live1 + s] = turned_ref[pl.ds(start, ROWS), :]
        return carry

    lax.fori_loop(0, live1, place, 0)


def pack(amps, ti, capt, across):
    return pl.pallas_call(
        functools.partial(pack_kernel, capt, across),
        in_specs=[SMEM, VMEM],
        out_specs=VMEM,
        scratch_shapes=[
            pltpu.VMEM((2 * capt * ROWS, LANES), F32),
            pltpu.VMEM((2 * capt * ROWS, LANES), BF16),
        ],
        out_shape=jax.ShapeDtypeStruct((LIVE2, ROWS, LANES), BF16),
        cost_estimate=pl.CostEstimate(flops=10**8, bytes_accessed=500000, transcendentals=0),
        name="pack_amps",
    )(ti, amps)


def prep_kernel(
    capt, across, nq, nmax, ti_ref, hbm_ref,
    meta_ref, mine_ref, send_ref, ints_ref, wide_ref, tab_ref, sem,
):
    fetch_ints = pltpu.make_async_copy(hbm_ref, ints_ref, sem)
    fetch_ints.start()
    dead = across * across
    me = lax.axis_index("pair")
    sibling = me ^ 1
    plane = lax.axis_index("reorder")
    second = plane * 2

    def build(which, who, k):
        def field(f):
            return (which * 5 + f) * nmax

        parity = lax.rem(k, 2)

        def one_first(q, cnt):
            i = (plane ^ q) * 2 + (who & 1)
            out = (lax.shift_right_logical(who, 1) ^ plane ^ q) * LIVE2
            for a in range(across + 1):
                tab_ref[a] = -1
            live_in = jnp.int32(0)
            for t in range(capt):
                idx = ti_ref[i, k, t]
                live_in = live_in + (idx < dead).astype(jnp.int32)
                a = row_of(idx, across)
                held = t * 32 + idx - a * across
                old = tab_ref[a]
                tab_ref[a] = jnp.where(old < 0, held, old)
                tab_ref[32 + a] = jnp.where(old < 0, -1, held)
            shift = q * LIVE2 + jnp.where(parity == 1, LIVE2 - live_in, 0)
            live1 = count_live(ti_ref, i, second + 1, capt, dead)
            for jj in range(2):
                for s in range(capt):
                    idx = ti_ref[i, second + jj, s]
                    a = row_of(idx, across)
                    b = idx - a * across
                    h0 = tab_ref[a]
                    h1 = tab_ref[32 + a]
                    hit = (idx < dead) & (h0 >= 0)
                    both = h1 >= 0
                    if which < 2:
                        place = out + (s if jj == 0 else LIVE2 - live1 + s)
                        meta_ref[field(0) + cnt] = place
                        t0 = shift + lax.shift_right_arithmetic(h0, 5)
                        t1 = shift + lax.shift_right_arithmetic(h1, 5)
                        meta_ref[field(1) + cnt] = t0
                        meta_ref[field(2) + cnt] = jnp.where(both, t1, t0)
                    if which != 1:
                        w0 = ((h0 & 31) * across + b) * 2 + jj
                        w1 = ((h1 & 31) * across + b) * 2 + jj
                        meta_ref[field(3) + cnt] = w0
                        meta_ref[field(4) + cnt] = jnp.where(both, w1, -1)
                    cnt = cnt + hit.astype(jnp.int32)
            return cnt

        total = lax.fori_loop(0, nq, one_first, jnp.int32(0))
        meta_ref[15 * nmax + which] = total
        return total

    def gather(which, total, tiles_ref):
        def fetch(step, carry):
            for u in range(4):
                e = jnp.minimum(step * 4 + u, total - 1)
                for m in range(2):
                    at = jnp.maximum(meta_ref[(which * 5 + 3 + m) * nmax + e], 0)
                    wide_ref[2 * u + m] = ints_ref[lax.shift_right_logical(at, 1)].astype(F32)
            for u in range(4):
                e = jnp.minimum(step * 4 + u, total - 1)
                for m in range(2):
                    at = meta_ref[(which * 5 + 3 + m) * nmax + e]
                    jj = jnp.maximum(at, 0) & 1
                    tile = wide_ref[2 * u + m, pl.ds(jj, ROWS, stride=2), :]
                    if m == 1:
                        tile = jnp.where(at >= 0, tile, 0.0)
                    tiles_ref[e, m * ROWS : (m + 1) * ROWS] = tile.astype(BF16)
            return carry

        lax.fori_loop(0, (total + 3) // 4, fetch, 0)

    total_send = build(2, sibling, me)
    total_mine = build(0, me, me)
    build(1, me, sibling)
    fetch_ints.wait()
    gather(2, total_send, send_ref)
    gather(0, total_mine, mine_ref)


def prep(cycle_ints, ti, capt, across, nq):
    nmax = nq * LIVE2 + 8
    ints = cycle_ints[0].transpose(1, 2, 0, 3).reshape(across, across, 2, ROWS, LANES)
    ints = ints.transpose(0, 1, 3, 2, 4).reshape(across * across, 2 * ROWS, LANES)
    tiles = jax.ShapeDtypeStruct((nq * LIVE2, 2 * ROWS, LANES), BF16)
    return pl.pallas_call(
        functools.partial(prep_kernel, capt, across, nq, nmax),
        in_specs=[SMEM, pl.BlockSpec(memory_space=pltpu.HBM)],
        out_specs=[SMEM, VMEM, VMEM],
        scratch_shapes=[
            pltpu.VMEM(ints.shape, BF16),
            pltpu.VMEM((8, 2 * ROWS, LANES), F32),
            pltpu.SMEM((64,), jnp.int32),
            pltpu.SemaphoreType.DMA,
        ],
        out_shape=[jax.ShapeDtypeStruct((15 * nmax + 8,), jnp.int32), tiles, tiles],
        compiler_params=pltpu.CompilerParams(vmem_limit_bytes=50 * 1024 * 1024),
        cost_estimate=pl.CostEstimate(flops=10**9, bytes_accessed=40 * 10**6, transcendentals=0),
        name="prep_integrals",
    )(ti, ints)


def denom_kernel(capt, across, ti_ref, slab_ref, occ_ref, vir_ref, inv_ref, row_ref, col_ref):
    first = lax.axis_index("pair")
    second = lax.axis_index("reorder") * 2
    occ_i = occ_ref[slab_ref[first]]
    low = lax.broadcasted_iota(jnp.int32, (8, LANES), 1) < 64
    for jj in range(2):
        for s in range(capt):
            idx = ti_ref[first, second + jj, s]
            row = row_of(idx, across)
            a = jnp.minimum(row, across - 1)
            b = idx - row * across
            row_ref[jj * capt + s] = vir_ref[a]
            col_ref[jj * capt + s] = vir_ref[b]
    for jj in range(2):
        occ = occ_i + occ_ref[slab_ref[second + jj]]
        for g in range(capt // 8):
            here = pl.ds(jj * capt + g * 8, 8)
            rows = occ - row_ref[here]
            col = col_ref[here]
            cols = jnp.concatenate([col, col], axis=1)
            for p in range(ROWS):
                even = jnp.broadcast_to(rows[:, 2 * p : 2 * p + 1], (8, LANES))
                odd = jnp.broadcast_to(rows[:, 2 * p + 1 : 2 * p + 2], (8, LANES))
                inv_ref[jj, g * 8 : (g + 1) * 8, p * LANES : (p + 1) * LANES] = 1.0 / (
                    jnp.where(low, even, odd) - cols
                )


def denominators(ti, slab, eps_occ, eps_vir, capt, across):
    return pl.pallas_call(
        functools.partial(denom_kernel, capt, across),
        in_specs=[SMEM, SMEM, SMEM, VMEM],
        out_specs=VMEM,
        scratch_shapes=[pltpu.VMEM((2 * capt, 64), F32)] * 2,
        out_shape=jax.ShapeDtypeStruct((2, capt, TILE * TILE), F32),
        cost_estimate=pl.CostEstimate(flops=10**7, bytes_accessed=10**6, transcendentals=0),
        name="denominators",
    )(ti, slab, eps_occ, eps_vir.reshape(across, 64))


def multiply_kernel(which, nq, nmax, unroll, meta_ref, tiles_ref, *refs):
    amps_refs, refs = refs[:nq], refs[nq:]
    if which == 0:
        sum_ref, amps_ref = refs
        sum_ref[...] = jnp.zeros(sum_ref.shape, F32)
    else:
        sum_ref, out_refs, amps_ref = refs[0], refs[1:-1], refs[-1]
    for q in range(nq):
        amps_ref[q * LIVE2 : (q + 1) * LIVE2] = amps_refs[q][...]
    low = lax.broadcasted_iota(jnp.int32, (ROWS, LANES), 1) < 64

    def spread(w):
        w = w.astype(F32)
        r = pltpu.roll(w, 64, 1)
        zero = jnp.zeros_like(w)
        parts = [
            jnp.where(low, w, zero),
            jnp.where(low, r, zero),
            jnp.where(low, zero, r),
            jnp.where(low, zero, w),
        ]
        return jnp.concatenate(parts, axis=0).astype(BF16)

    total = meta_ref[15 * nmax + which]

    def several(step, carry):
        results = []
        for u in range(unroll):
            e = jnp.minimum(step * unroll + u, total - 1)
            at = which * 5 * nmax + e
            left = jnp.concatenate(
                [amps_ref[meta_ref[nmax + at]], amps_ref[meta_ref[2 * nmax + at]]], axis=1
            )
            right = jnp.concatenate(
                [spread(tiles_ref[e, 0:ROWS]), spread(tiles_ref[e, ROWS : 2 * ROWS])], axis=0
            )
            place = jnp.where(step * unroll + u < total, meta_ref[at], nq * LIVE2)
            results.append((place, jnp.dot(left, right, preferred_element_type=F32)))
        for place, value in results:
            if which == 0:
                sum_ref[place] = value
            else:
                sum_ref[place] += value
        return carry

    lax.fori_loop(0, (total + unroll - 1) // unroll, several, 0)
    if which == 1:
        for q in range(nq):
            out_refs[q][...] = sum_ref[q * LIVE2 : (q + 1) * LIVE2].astype(BF16)


def multiply(which, meta, tiles, amps, sums, nq):
    block = jax.ShapeDtypeStruct((LIVE2, ROWS, LANES), BF16)
    total = jax.ShapeDtypeStruct((nq * LIVE2 + 1, ROWS, LANES), F32)
    out = [block] * nq if which == 1 else total
    return pl.pallas_call(
        functools.partial(multiply_kernel, which, nq, nq * LIVE2 + 8, 8),
        in_specs=[SMEM] + [VMEM] * (1 + len(amps) + len(sums)),
        out_specs=jax.tree.map(lambda _: VMEM, out),
        out_shape=out,
        scratch_shapes=[pltpu.VMEM((nq * LIVE2, ROWS, LANES), BF16)],
        compiler_params=pltpu.CompilerParams(vmem_limit_bytes=24 * 1024 * 1024),
        cost_estimate=pl.CostEstimate(flops=10**9, bytes_accessed=6 * 10**6, transcendentals=0),
        name=("multiply_own", "multiply_sibling")[which],
    )(meta, tiles, *amps, *sums)


def update_kernel(
    capt, across, nq, ti_ref, amps_ref, ovov_ref, hist_ref, inv_ref, *refs
):
    part_refs, (new_ref, gram_ref, sum_ref, total_ref) = refs[:nq], refs[nq:]
    nhist = hist_ref.shape[0]
    first = lax.axis_index("pair")
    second = lax.axis_index("reorder") * 2

    def add(s, carry):
        acc = part_refs[0][s].astype(F32)
        for part_ref in part_refs[1:]:
            acc = acc + part_ref[s].astype(F32)
        sum_ref[pl.ds(pl.multiple_of(s * ROWS, ROWS), ROWS), :] = acc
        return carry

    lax.fori_loop(0, LIVE2, add, 0, unroll=4)
    slot = lax.broadcasted_iota(jnp.int32, (capt, LANES), 0)
    accs = [jnp.zeros((capt, LANES), F32) for _ in range(nhist + 1)]
    for jj in range(2):
        count = count_live(ti_ref, first, second + jj, capt, across * across)
        start = 0 if jj == 0 else (LIVE2 - count) * ROWS
        alive = slot < count

        def chunk(p, accs):
            here = pl.ds(pl.multiple_of(p * LANES, LANES), LANES)
            cycle = jnp.concatenate(
                [
                    sum_ref[pl.ds(start + g * ROWS + p, 8, stride=ROWS), :]
                    for g in range(0, capt, 8)
                ],
                axis=0,
            )
            resid = jnp.where(alive, ovov_ref[0, jj, :, here].astype(F32) + cycle, 0.0)
            moved = amps_ref[0, jj, :, here].astype(F32) + resid * inv_ref[jj, :, here]
            new_ref[0, jj, :, here] = jnp.where(alive, moved, 0.0).astype(BF16)
            out = [
                accs[m] + hist_ref[m, 0, jj, :, here].astype(F32) * resid for m in range(nhist)
            ]
            out.append(accs[nhist] + resid * resid)
            return out

        accs = lax.fori_loop(0, ROWS, chunk, accs, unroll=4)
    for m in range(8):
        row = jnp.zeros((1, LANES), F32)
        if m <= nhist:
            row = jnp.sum(accs[m], axis=0, keepdims=True)
        total_ref[m : m + 1] = row
    gram_ref[...] = jnp.broadcast_to(total_ref[...][None], gram_ref.shape)


def update(ti, amps, ovov, history, inv, parts, copies, capt, across):
    nq = len(parts)
    return pl.pallas_call(
        functools.partial(update_kernel, capt, across, nq),
        in_specs=[SMEM] + [VMEM] * (4 + nq),
        out_specs=[VMEM, VMEM],
        out_shape=[
            jax.ShapeDtypeStruct(amps.shape, BF16),
            jax.ShapeDtypeStruct((copies, 8, LANES), F32),
        ],
        scratch_shapes=[
            pltpu.VMEM(((LIVE2 + capt) * ROWS, LANES), F32),
            pltpu.VMEM((8, LANES), F32),
        ],
        compiler_params=pltpu.CompilerParams(vmem_limit_bytes=24 * 1024 * 1024),
        cost_estimate=pl.CostEstimate(flops=10**8, bytes_accessed=6 * 10**6, transcendentals=0),
        name="update_amps",
    )(ti, amps, ovov, history, inv, *parts)


def finish_kernel(nhist, scale, sums_ref, out_ref):
    total = jnp.sum(sums_ref[...], axis=0)
    total = jnp.sum(total, axis=1, keepdims=True)
    row = lax.broadcasted_iota(jnp.int32, total.shape, 0)
    total = jnp.where(row == nhist, jnp.sqrt(jnp.maximum(total, 0.0)), total) * scale
    for m in range(nhist + 1):
        out_ref[m] = total[m, 0]


def finish(sums, nhist, scale):
    return pl.pallas_call(
        functools.partial(finish_kernel, nhist, scale),
        in_specs=[VMEM],
        out_specs=SMEM,
        out_shape=jax.ShapeDtypeStruct((nhist + 1,), F32),
        name="finish_gram",
    )(sums)


def swap(x, axis, size, step):
    return lax.ppermute(x, axis, [(n, n ^ step) for n in range(size)])


def spread_perm(npair, nq, m):
    return [
        (z * npair + p, ((p // 2) ^ m) * npair + 2 * z + p % 2)
        for z in range(nq)
        for p in range(npair)
    ]


def local(npair, nq, amps, tile_index, ovov, cycle_ints, history, slab, eps_occ, eps_vir):
    occ_dev, jdev, capt, tile_area = amps.shape
    ns = tile_index.shape[0]
    across = cycle_ints.shape[2]
    nhist = history.shape[0]
    assert occ_dev == 1 and jdev == 2 and tile_area == TILE * TILE and capt == 16
    assert ns == npair == 2 * nq
    packed = pack(amps, tile_index, capt, across)
    axes = ("reorder", "pair")
    turned = [lax.ppermute(packed, axes, spread_perm(npair, nq, m)) for m in range(nq)]
    late = lax.optimization_barrier((packed, cycle_ints, tile_index, slab, eps_occ, eps_vir))
    meta, mine, send = prep(*late[1:3], capt, across, nq)
    inv = denominators(*late[2:], capt, across)
    turned, send, inv = lax.optimization_barrier((turned, send, inv))
    theirs = swap(send, "pair", npair, 1)
    sums = multiply(0, meta, mine, turned, [], nq)
    partial = multiply(1, meta, theirs, turned, [sums], nq)
    parts = [partial[0]] + [swap(partial[e], "pair", npair, 2 * e) for e in range(1, nq)]
    new_amps, gram = update(
        tile_index, amps, ovov, history, inv, parts, npair * nq, capt, across
    )
    sums = lax.all_to_all(gram, axes, split_axis=0, concat_axis=0, tiled=True)
    return (new_amps, finish(sums, nhist, 1.0 / (TILE * ns)))


def solution(mesh):
    in_specs = (
        P("pair", "reorder", None, None),
        P(),
        P("pair", "reorder", None, None),
        P("pair", "reorder", None, None, None),
        P(None, "pair", "reorder", None, None),
        P(),
        P(),
        P(),
    )
    out_specs = (P("pair", "reorder", None, None), P())
    body = functools.partial(local, mesh.shape["pair"], mesh.shape["reorder"])
    return jax.shard_map(body, mesh=mesh, in_specs=in_specs, out_specs=out_specs, check_vma=False)
```

```python
import functools

import jax
import jax.numpy as jnp
from jax import lax
from jax.experimental import pallas as pl
from jax.experimental.pallas import tpu as pltpu
from jax.sharding import PartitionSpec as P

TILE = 64
ROWS = 32
LANES = 128
LIVE2 = 24
F32 = jnp.float32
BF16 = jnp.bfloat16
SMEM = pl.BlockSpec(memory_space=pltpu.SMEM)
VMEM = pl.BlockSpec(memory_space=pltpu.VMEM)


def count_live(ti_ref, i, j, capt, dead):
    total = jnp.int32(0)
    for s in range(capt):
        total = total + (ti_ref[i, j, s] < dead).astype(jnp.int32)
    return total


def row_of(idx, across):
    factor = -(-(1 << 17) // across)
    assert all((n * factor) >> 17 == n // across for n in range(across * across + 1))
    return lax.shift_right_logical(idx * factor, 17)


def pack_kernel(capt, across, ti_ref, amps_ref, out_ref, flat_ref, turned_ref):
    first = lax.axis_index("pair")
    second = lax.axis_index("reorder") * 2
    live1 = count_live(ti_ref, first, second + 1, capt, across * across)
    for jj in range(2):
        for p in range(ROWS):
            chunk = amps_ref[0, jj, :, p * LANES : (p + 1) * LANES].astype(F32)
            for g in range(capt // 8):
                start = (jj * capt + g * 8) * ROWS + p
                flat_ref[pl.ds(start, 8, stride=ROWS), :] = chunk[g * 8 : (g + 1) * 8]
    old = lax.broadcasted_iota(jnp.int32, (LANES, LANES), 0)
    new = lax.broadcasted_iota(jnp.int32, (LANES, LANES), 1)
    source = (new // 64) * 64 + (new % 32) * 2 + (new % 64) // 32
    turn = (old == source).astype(F32).astype(BF16)
    turned_ref[...] = jnp.dot(
        flat_ref[...].astype(BF16), turn, preferred_element_type=F32
    ).astype(BF16)
    out_ref[0:capt] = turned_ref[0 : capt * ROWS].reshape(capt, ROWS, LANES)
    out_ref[capt:LIVE2] = jnp.zeros((LIVE2 - capt, ROWS, LANES), BF16)

    def place(s, carry):
        start = pl.multiple_of((capt + s) * ROWS, ROWS)
        out_ref[LIVE2 - live1 + s] = turned_ref[pl.ds(start, ROWS), :]
        return carry

    lax.fori_loop(0, live1, place, 0)


def pack(amps, ti, capt, across):
    return pl.pallas_call(
        functools.partial(pack_kernel, capt, across),
        in_specs=[SMEM, VMEM],
        out_specs=VMEM,
        scratch_shapes=[
            pltpu.VMEM((2 * capt * ROWS, LANES), F32),
            pltpu.VMEM((2 * capt * ROWS, LANES), BF16),
        ],
        out_shape=jax.ShapeDtypeStruct((LIVE2, ROWS, LANES), BF16),
        cost_estimate=pl.CostEstimate(flops=10**8, bytes_accessed=500000, transcendentals=0),
        name="pack_amps",
    )(ti, amps)


def prep_kernel(
    capt, across, nq, nmax, ti_ref, hbm_ref,
    meta_ref, mine_ref, send_ref, ints_ref, wide_ref, tab_ref, sem,
):
    fetch_ints = pltpu.make_async_copy(hbm_ref, ints_ref, sem)
    fetch_ints.start()
    dead = across * across
    me = lax.axis_index("pair")
    sibling = me ^ 1
    plane = lax.axis_index("reorder")
    second = plane * 2

    def build(which, who, k):
        def field(f):
            return (which * 5 + f) * nmax

        parity = lax.rem(k, 2)

        def one_first(q, cnt):
            i = (plane ^ q) * 2 + (who & 1)
            out = (lax.shift_right_logical(who, 1) ^ plane ^ q) * LIVE2
            for a in range(across + 1):
                tab_ref[a] = -1
            live_in = jnp.int32(0)
            for t in range(capt):
                idx = ti_ref[i, k, t]
                live_in = live_in + (idx < dead).astype(jnp.int32)
                a = row_of(idx, across)
                held = t * 32 + idx - a * across
                old = tab_ref[a]
                tab_ref[a] = jnp.where(old < 0, held, old)
                tab_ref[32 + a] = jnp.where(old < 0, -1, held)
            shift = q * LIVE2 + jnp.where(parity == 1, LIVE2 - live_in, 0)
            live1 = count_live(ti_ref, i, second + 1, capt, dead)
            for jj in range(2):
                for s in range(capt):
                    idx = ti_ref[i, second + jj, s]
                    a = row_of(idx, across)
                    b = idx - a * across
                    h0 = tab_ref[a]
                    h1 = tab_ref[32 + a]
                    hit = (idx < dead) & (h0 >= 0)
                    both = h1 >= 0
                    if which < 2:
                        place = out + (s if jj == 0 else LIVE2 - live1 + s)
                        meta_ref[field(0) + cnt] = place
                        t0 = shift + lax.shift_right_arithmetic(h0, 5)
                        t1 = shift + lax.shift_right_arithmetic(h1, 5)
                        meta_ref[field(1) + cnt] = t0
                        meta_ref[field(2) + cnt] = jnp.where(both, t1, t0)
                    if which != 1:
                        w0 = ((h0 & 31) * across + b) * 2 + jj
                        w1 = ((h1 & 31) * across + b) * 2 + jj
                        meta_ref[field(3) + cnt] = w0
                        meta_ref[field(4) + cnt] = jnp.where(both, w1, -1)
                    cnt = cnt + hit.astype(jnp.int32)
            return cnt

        total = lax.fori_loop(0, nq, one_first, jnp.int32(0))
        meta_ref[15 * nmax + which] = total
        return total

    def gather(which, total, tiles_ref):
        def fetch(step, carry):
            for u in range(4):
                e = jnp.minimum(step * 4 + u, total - 1)
                for m in range(2):
                    at = jnp.maximum(meta_ref[(which * 5 + 3 + m) * nmax + e], 0)
                    wide_ref[2 * u + m] = ints_ref[lax.shift_right_logical(at, 1)].astype(F32)
            for u in range(4):
                e = jnp.minimum(step * 4 + u, total - 1)
                for m in range(2):
                    at = meta_ref[(which * 5 + 3 + m) * nmax + e]
                    jj = jnp.maximum(at, 0) & 1
                    tile = wide_ref[2 * u + m, pl.ds(jj, ROWS, stride=2), :]
                    if m == 1:
                        tile = jnp.where(at >= 0, tile, 0.0)
                    tiles_ref[e, m * ROWS : (m + 1) * ROWS] = tile.astype(BF16)
            return carry

        lax.fori_loop(0, (total + 3) // 4, fetch, 0)

    total_send = build(2, sibling, me)
    total_mine = build(0, me, me)
    build(1, me, sibling)
    fetch_ints.wait()
    gather(2, total_send, send_ref)
    gather(0, total_mine, mine_ref)


def prep(cycle_ints, ti, capt, across, nq):
    nmax = nq * LIVE2 + 8
    ints = cycle_ints[0].transpose(1, 2, 0, 3).reshape(across, across, 2, ROWS, LANES)
    ints = ints.transpose(0, 1, 3, 2, 4).reshape(across * across, 2 * ROWS, LANES)
    tiles = jax.ShapeDtypeStruct((nq * LIVE2, 2 * ROWS, LANES), BF16)
    return pl.pallas_call(
        functools.partial(prep_kernel, capt, across, nq, nmax),
        in_specs=[SMEM, pl.BlockSpec(memory_space=pltpu.HBM)],
        out_specs=[SMEM, VMEM, VMEM],
        scratch_shapes=[
            pltpu.VMEM(ints.shape, BF16),
            pltpu.VMEM((8, 2 * ROWS, LANES), F32),
            pltpu.SMEM((64,), jnp.int32),
            pltpu.SemaphoreType.DMA,
        ],
        out_shape=[jax.ShapeDtypeStruct((15 * nmax + 8,), jnp.int32), tiles, tiles],
        compiler_params=pltpu.CompilerParams(vmem_limit_bytes=50 * 1024 * 1024),
        cost_estimate=pl.CostEstimate(flops=10**9, bytes_accessed=40 * 10**6, transcendentals=0),
        name="prep_integrals",
    )(ti, ints)


def denom_kernel(capt, across, ti_ref, slab_ref, occ_ref, vir_ref, inv_ref, row_ref, col_ref):
    first = lax.axis_index("pair")
    second = lax.axis_index("reorder") * 2
    occ_i = occ_ref[slab_ref[first]]
    low = lax.broadcasted_iota(jnp.int32, (8, LANES), 1) < 64
    for jj in range(2):
        for s in range(capt):
            idx = ti_ref[first, second + jj, s]
            row = row_of(idx, across)
            a = jnp.minimum(row, across - 1)
            b = idx - row * across
            row_ref[jj * capt + s] = vir_ref[a]
            col_ref[jj * capt + s] = vir_ref[b]
    for jj in range(2):
        occ = occ_i + occ_ref[slab_ref[second + jj]]
        for g in range(capt // 8):
            here = pl.ds(jj * capt + g * 8, 8)
            rows = occ - row_ref[here]
            col = col_ref[here]
            cols = jnp.concatenate([col, col], axis=1)
            for p in range(ROWS):
                even = jnp.broadcast_to(rows[:, 2 * p : 2 * p + 1], (8, LANES))
                odd = jnp.broadcast_to(rows[:, 2 * p + 1 : 2 * p + 2], (8, LANES))
                inv_ref[jj, g * 8 : (g + 1) * 8, p * LANES : (p + 1) * LANES] = 1.0 / (
                    jnp.where(low, even, odd) - cols
                )


def denominators(ti, slab, eps_occ, eps_vir, capt, across):
    return pl.pallas_call(
        functools.partial(denom_kernel, capt, across),
        in_specs=[SMEM, SMEM, SMEM, VMEM],
        out_specs=VMEM,
        scratch_shapes=[pltpu.VMEM((2 * capt, 64), F32)] * 2,
        out_shape=jax.ShapeDtypeStruct((2, capt, TILE * TILE), F32),
        cost_estimate=pl.CostEstimate(flops=10**7, bytes_accessed=10**6, transcendentals=0),
        name="denominators",
    )(ti, slab, eps_occ, eps_vir.reshape(across, 64))


def multiply_kernel(which, nq, nmax, unroll, meta_ref, tiles_ref, *refs):
    amps_refs, refs = refs[:nq], refs[nq:]
    if which == 0:
        sum_ref, amps_ref = refs
        sum_ref[...] = jnp.zeros(sum_ref.shape, F32)
    else:
        sum_ref, out_refs, amps_ref = refs[0], refs[1:-1], refs[-1]
    for q in range(nq):
        amps_ref[q * LIVE2 : (q + 1) * LIVE2] = amps_refs[q][...]
    low = lax.broadcasted_iota(jnp.int32, (ROWS, LANES), 1) < 64

    def spread(w):
        w = w.astype(F32)
        r = pltpu.roll(w, 64, 1)
        zero = jnp.zeros_like(w)
        parts = [
            jnp.where(low, w, zero),
            jnp.where(low, r, zero),
            jnp.where(low, zero, r),
            jnp.where(low, zero, w),
        ]
        return jnp.concatenate(parts, axis=0).astype(BF16)

    total = meta_ref[15 * nmax + which]

    def several(step, carry):
        results = []
        for u in range(unroll):
            e = jnp.minimum(step * unroll + u, total - 1)
            at = which * 5 * nmax + e
            left = jnp.concatenate(
                [amps_ref[meta_ref[nmax + at]], amps_ref[meta_ref[2 * nmax + at]]], axis=1
            )
            right = jnp.concatenate(
                [spread(tiles_ref[e, 0:ROWS]), spread(tiles_ref[e, ROWS : 2 * ROWS])], axis=0
            )
            place = jnp.where(step * unroll + u < total, meta_ref[at], nq * LIVE2)
            results.append((place, jnp.dot(left, right, preferred_element_type=F32)))
        for place, value in results:
            if which == 0:
                sum_ref[place] = value
            else:
                sum_ref[place] += value
        return carry

    lax.fori_loop(0, (total + unroll - 1) // unroll, several, 0)
    if which == 1:
        for q in range(nq):
            out_refs[q][...] = sum_ref[q * LIVE2 : (q + 1) * LIVE2].astype(BF16)


def multiply(which, meta, tiles, amps, sums, nq):
    block = jax.ShapeDtypeStruct((LIVE2, ROWS, LANES), BF16)
    total = jax.ShapeDtypeStruct((nq * LIVE2 + 1, ROWS, LANES), F32)
    out = [block] * nq if which == 1 else total
    return pl.pallas_call(
        functools.partial(multiply_kernel, which, nq, nq * LIVE2 + 8, 8),
        in_specs=[SMEM] + [VMEM] * (1 + len(amps) + len(sums)),
        out_specs=jax.tree.map(lambda _: VMEM, out),
        out_shape=out,
        scratch_shapes=[pltpu.VMEM((nq * LIVE2, ROWS, LANES), BF16)],
        compiler_params=pltpu.CompilerParams(vmem_limit_bytes=24 * 1024 * 1024),
        cost_estimate=pl.CostEstimate(flops=10**9, bytes_accessed=6 * 10**6, transcendentals=0),
        name=("multiply_own", "multiply_sibling")[which],
    )(meta, tiles, *amps, *sums)


def update_kernel(
    capt, across, nq, ti_ref, amps_ref, ovov_ref, hist_ref, inv_ref, *refs
):
    part_refs, (new_ref, gram_ref, sum_ref) = refs[:nq], refs[nq:]
    nhist = hist_ref.shape[0]
    first = lax.axis_index("pair")
    second = lax.axis_index("reorder") * 2

    def add(s, carry):
        acc = part_refs[0][s].astype(F32)
        for part_ref in part_refs[1:]:
            acc = acc + part_ref[s].astype(F32)
        sum_ref[pl.ds(pl.multiple_of(s * ROWS, ROWS), ROWS), :] = acc
        return carry

    lax.fori_loop(0, LIVE2, add, 0, unroll=4)
    slot = lax.broadcasted_iota(jnp.int32, (8, LANES), 0)
    accs = [jnp.zeros((8, LANES), F32) for _ in range(nhist + 1)]
    for jj in range(2):
        count = count_live(ti_ref, first, second + jj, capt, across * across)
        start = 0 if jj == 0 else (LIVE2 - count) * ROWS
        for g in range(capt // 8):
            alive = slot + g * 8 < count
            rows = slice(g * 8, (g + 1) * 8)

            def chunk(p, accs):
                here = pl.ds(pl.multiple_of(p * LANES, LANES), LANES)
                cycle = sum_ref[pl.ds(start + g * 8 * ROWS + p, 8, stride=ROWS), :]
                resid = jnp.where(alive, ovov_ref[0, jj, rows, here].astype(F32) + cycle, 0.0)
                moved = amps_ref[0, jj, rows, here].astype(F32) + resid * inv_ref[jj, rows, here]
                new_ref[0, jj, rows, here] = jnp.where(alive, moved, 0.0).astype(BF16)
                out = [
                    accs[m] + hist_ref[m, 0, jj, rows, here].astype(F32) * resid
                    for m in range(nhist)
                ]
                out.append(accs[nhist] + resid * resid)
                return out

            accs = lax.fori_loop(0, ROWS, chunk, accs, unroll=8)
    lane = lax.broadcasted_iota(jnp.int32, (1, LANES), 1)
    row = jnp.zeros((1, LANES), F32)
    for m in range(nhist + 1):
        row = jnp.where(lane == m, jnp.sum(accs[m]), row)
    for n in range(gram_ref.shape[0]):
        gram_ref[n] = row


def update(ti, amps, ovov, history, inv, parts, copies, capt, across):
    nq = len(parts)
    return pl.pallas_call(
        functools.partial(update_kernel, capt, across, nq),
        in_specs=[SMEM] + [VMEM] * (4 + nq),
        out_specs=[VMEM, VMEM],
        out_shape=[
            jax.ShapeDtypeStruct(amps.shape, BF16),
            jax.ShapeDtypeStruct((copies, 1, LANES), F32),
        ],
        scratch_shapes=[
            pltpu.VMEM(((LIVE2 + capt) * ROWS, LANES), F32),
        ],
        compiler_params=pltpu.CompilerParams(vmem_limit_bytes=24 * 1024 * 1024),
        cost_estimate=pl.CostEstimate(flops=10**8, bytes_accessed=6 * 10**6, transcendentals=0),
        name="update_amps",
    )(ti, amps, ovov, history, inv, *parts)


def finish_kernel(nhist, scale, sums_ref, out_ref):
    total = sums_ref[0]
    for n in range(1, sums_ref.shape[0]):
        total = total + sums_ref[n]
    lane = lax.broadcasted_iota(jnp.int32, total.shape, 1)
    total = jnp.where(lane == nhist, jnp.sqrt(jnp.maximum(total, 0.0)), total) * scale
    for m in range(nhist + 1):
        out_ref[m] = total[0, m]


def finish(sums, nhist, scale):
    return pl.pallas_call(
        functools.partial(finish_kernel, nhist, scale),
        in_specs=[VMEM],
        out_specs=SMEM,
        out_shape=jax.ShapeDtypeStruct((nhist + 1,), F32),
        name="finish_gram",
    )(sums)


def swap(x, axis, size, step):
    return lax.ppermute(x, axis, [(n, n ^ step) for n in range(size)])


def spread_perm(npair, nq, m):
    return [
        (z * npair + p, ((p // 2) ^ m) * npair + 2 * z + p % 2)
        for z in range(nq)
        for p in range(npair)
    ]


def local(npair, nq, amps, tile_index, ovov, cycle_ints, history, slab, eps_occ, eps_vir):
    occ_dev, jdev, capt, tile_area = amps.shape
    ns = tile_index.shape[0]
    across = cycle_ints.shape[2]
    nhist = history.shape[0]
    assert occ_dev == 1 and jdev == 2 and tile_area == TILE * TILE and capt == 16
    assert ns == npair == 2 * nq
    packed = pack(amps, tile_index, capt, across)
    axes = ("reorder", "pair")
    turned = [lax.ppermute(packed, axes, spread_perm(npair, nq, m)) for m in range(nq)]
    late = lax.optimization_barrier((packed, cycle_ints, tile_index, slab, eps_occ, eps_vir))
    meta, mine, send = prep(*late[1:3], capt, across, nq)
    inv = denominators(*late[2:], capt, across)
    turned, send, inv = lax.optimization_barrier((turned, send, inv))
    theirs = swap(send, "pair", npair, 1)
    sums = multiply(0, meta, mine, turned, [], nq)
    partial = multiply(1, meta, theirs, turned, [sums], nq)
    parts = [partial[0]] + [swap(partial[e], "pair", npair, 2 * e) for e in range(1, nq)]
    new_amps, gram = update(
        tile_index, amps, ovov, history, inv, parts, npair * nq, capt, across
    )
    sums = lax.all_to_all(gram, axes, split_axis=0, concat_axis=0, tiled=True)
    return (new_amps, finish(sums, nhist, 1.0 / (TILE * ns)))


def solution(mesh):
    in_specs = (
        P("pair", "reorder", None, None),
        P(),
        P("pair", "reorder", None, None),
        P("pair", "reorder", None, None, None),
        P(None, "pair", "reorder", None, None),
        P(),
        P(),
        P(),
    )
    out_specs = (P("pair", "reorder", None, None), P())
    body = functools.partial(local, mesh.shape["pair"], mesh.shape["reorder"])
    return jax.shard_map(body, mesh=mesh, in_specs=in_specs, out_specs=out_specs, check_vma=False)
```

```python
import functools

import jax
import jax.numpy as jnp
from jax import lax
from jax.experimental import pallas as pl
from jax.experimental.pallas import tpu as pltpu
from jax.sharding import PartitionSpec as P

TILE = 64
ROWS = 32
LANES = 128
LIVE2 = 24
F32 = jnp.float32
BF16 = jnp.bfloat16
SMEM = pl.BlockSpec(memory_space=pltpu.SMEM)
VMEM = pl.BlockSpec(memory_space=pltpu.VMEM)


def count_live(ti_ref, i, j, capt, dead):
    total = jnp.int32(0)
    for s in range(capt):
        total = total + (ti_ref[i, j, s] < dead).astype(jnp.int32)
    return total


def row_of(idx, across):
    factor = -(-(1 << 17) // across)
    assert all((n * factor) >> 17 == n // across for n in range(across * across + 1))
    return lax.shift_right_logical(idx * factor, 17)


def pack_kernel(capt, across, ti_ref, amps_ref, out_ref, flat_ref, turned_ref):
    first = lax.axis_index("pair")
    second = lax.axis_index("reorder") * 2
    live1 = count_live(ti_ref, first, second + 1, capt, across * across)
    for jj in range(2):
        for p in range(ROWS):
            chunk = amps_ref[0, jj, :, p * LANES : (p + 1) * LANES].astype(F32)
            for g in range(capt // 8):
                start = (jj * capt + g * 8) * ROWS + p
                flat_ref[pl.ds(start, 8, stride=ROWS), :] = chunk[g * 8 : (g + 1) * 8]
    old = lax.broadcasted_iota(jnp.int32, (LANES, LANES), 0)
    new = lax.broadcasted_iota(jnp.int32, (LANES, LANES), 1)
    source = (new // 64) * 64 + (new % 32) * 2 + (new % 64) // 32
    turn = (old == source).astype(F32).astype(BF16)
    turned_ref[...] = jnp.dot(
        flat_ref[...].astype(BF16), turn, preferred_element_type=F32
    ).astype(BF16)
    out_ref[0:capt] = turned_ref[0 : capt * ROWS].reshape(capt, ROWS, LANES)
    out_ref[capt:LIVE2] = jnp.zeros((LIVE2 - capt, ROWS, LANES), BF16)

    def place(s, carry):
        start = pl.multiple_of((capt + s) * ROWS, ROWS)
        out_ref[LIVE2 - live1 + s] = turned_ref[pl.ds(start, ROWS), :]
        return carry

    lax.fori_loop(0, live1, place, 0)


def pack(amps, ti, capt, across):
    return pl.pallas_call(
        functools.partial(pack_kernel, capt, across),
        in_specs=[SMEM, VMEM],
        out_specs=VMEM,
        scratch_shapes=[
            pltpu.VMEM((2 * capt * ROWS, LANES), F32),
            pltpu.VMEM((2 * capt * ROWS, LANES), BF16),
        ],
        out_shape=jax.ShapeDtypeStruct((LIVE2, ROWS, LANES), BF16),
        cost_estimate=pl.CostEstimate(flops=10**8, bytes_accessed=500000, transcendentals=0),
        name="pack_amps",
    )(ti, amps)


def prep_kernel(
    capt, across, nq, nmax, ti_ref, hbm_ref,
    meta_ref, mine_ref, send_ref, ints_ref, wide_ref, tab_ref, sem,
):
    fetch_ints = pltpu.make_async_copy(hbm_ref, ints_ref, sem)
    fetch_ints.start()
    dead = across * across
    me = lax.axis_index("pair")
    sibling = me ^ 1
    plane = lax.axis_index("reorder")
    second = plane * 2

    def build(which, who, k):
        def field(f):
            return (which * 5 + f) * nmax

        parity = lax.rem(k, 2)

        def one_first(q, cnt):
            i = (plane ^ q) * 2 + (who & 1)
            out = (lax.shift_right_logical(who, 1) ^ plane ^ q) * LIVE2
            for a in range(across + 1):
                tab_ref[a] = -1
            live_in = jnp.int32(0)
            for t in range(capt):
                idx = ti_ref[i, k, t]
                live_in = live_in + (idx < dead).astype(jnp.int32)
                a = row_of(idx, across)
                held = t * 32 + idx - a * across
                old = tab_ref[a]
                tab_ref[a] = jnp.where(old < 0, held, old)
                tab_ref[32 + a] = jnp.where(old < 0, -1, held)
            shift = q * LIVE2 + jnp.where(parity == 1, LIVE2 - live_in, 0)
            live1 = count_live(ti_ref, i, second + 1, capt, dead)
            for jj in range(2):
                for s in range(capt):
                    idx = ti_ref[i, second + jj, s]
                    a = row_of(idx, across)
                    b = idx - a * across
                    h0 = tab_ref[a]
                    h1 = tab_ref[32 + a]
                    hit = (idx < dead) & (h0 >= 0)
                    both = h1 >= 0
                    if which < 2:
                        place = out + (s if jj == 0 else LIVE2 - live1 + s)
                        meta_ref[field(0) + cnt] = place
                        t0 = shift + lax.shift_right_arithmetic(h0, 5)
                        t1 = shift + lax.shift_right_arithmetic(h1, 5)
                        meta_ref[field(1) + cnt] = t0
                        meta_ref[field(2) + cnt] = jnp.where(both, t1, t0)
                    if which != 1:
                        w0 = ((h0 & 31) * across + b) * 2 + jj
                        w1 = ((h1 & 31) * across + b) * 2 + jj
                        meta_ref[field(3) + cnt] = w0
                        meta_ref[field(4) + cnt] = jnp.where(both, w1, -1)
                    cnt = cnt + hit.astype(jnp.int32)
            return cnt

        total = lax.fori_loop(0, nq, one_first, jnp.int32(0))
        meta_ref[15 * nmax + which] = total
        return total

    def gather(which, total, tiles_ref):
        def fetch(step, carry):
            for u in range(4):
                e = jnp.minimum(step * 4 + u, total - 1)
                for m in range(2):
                    at = jnp.maximum(meta_ref[(which * 5 + 3 + m) * nmax + e], 0)
                    wide_ref[2 * u + m] = ints_ref[lax.shift_right_logical(at, 1)].astype(F32)
            for u in range(4):
                e = jnp.minimum(step * 4 + u, total - 1)
                for m in range(2):
                    at = meta_ref[(which * 5 + 3 + m) * nmax + e]
                    jj = jnp.maximum(at, 0) & 1
                    tile = wide_ref[2 * u + m, pl.ds(jj, ROWS, stride=2), :]
                    if m == 1:
                        tile = jnp.where(at >= 0, tile, 0.0)
                    tiles_ref[e, m * ROWS : (m + 1) * ROWS] = tile.astype(BF16)
            return carry

        lax.fori_loop(0, (total + 3) // 4, fetch, 0)

    total_send = build(2, sibling, me)
    total_mine = build(0, me, me)
    build(1, me, sibling)
    fetch_ints.wait()
    gather(2, total_send, send_ref)
    gather(0, total_mine, mine_ref)


def prep(cycle_ints, ti, capt, across, nq):
    nmax = nq * LIVE2 + 8
    ints = cycle_ints[0].transpose(1, 2, 0, 3).reshape(across, across, 2, ROWS, LANES)
    ints = ints.transpose(0, 1, 3, 2, 4).reshape(across * across, 2 * ROWS, LANES)
    tiles = jax.ShapeDtypeStruct((nq * LIVE2, 2 * ROWS, LANES), BF16)
    return pl.pallas_call(
        functools.partial(prep_kernel, capt, across, nq, nmax),
        in_specs=[SMEM, pl.BlockSpec(memory_space=pltpu.HBM)],
        out_specs=[SMEM, VMEM, VMEM],
        scratch_shapes=[
            pltpu.VMEM(ints.shape, BF16),
            pltpu.VMEM((8, 2 * ROWS, LANES), F32),
            pltpu.SMEM((64,), jnp.int32),
            pltpu.SemaphoreType.DMA,
        ],
        out_shape=[jax.ShapeDtypeStruct((15 * nmax + 8,), jnp.int32), tiles, tiles],
        compiler_params=pltpu.CompilerParams(vmem_limit_bytes=50 * 1024 * 1024),
        cost_estimate=pl.CostEstimate(flops=10**9, bytes_accessed=40 * 10**6, transcendentals=0),
        name="prep_integrals",
    )(ti, ints)


def denom_kernel(capt, across, ti_ref, slab_ref, occ_ref, vir_ref, inv_ref, row_ref, col_ref):
    first = lax.axis_index("pair")
    second = lax.axis_index("reorder") * 2
    occ_i = occ_ref[slab_ref[first]]
    low = lax.broadcasted_iota(jnp.int32, (8, LANES), 1) < 64
    for jj in range(2):
        for s in range(capt):
            idx = ti_ref[first, second + jj, s]
            row = row_of(idx, across)
            a = jnp.minimum(row, across - 1)
            b = idx - row * across
            row_ref[jj * capt + s] = vir_ref[a]
            col_ref[jj * capt + s] = vir_ref[b]
    for jj in range(2):
        occ = occ_i + occ_ref[slab_ref[second + jj]]
        for g in range(capt // 8):
            here = pl.ds(jj * capt + g * 8, 8)
            rows = occ - row_ref[here]
            col = col_ref[here]
            cols = jnp.concatenate([col, col], axis=1)
            for p in range(ROWS):
                even = jnp.broadcast_to(rows[:, 2 * p : 2 * p + 1], (8, LANES))
                odd = jnp.broadcast_to(rows[:, 2 * p + 1 : 2 * p + 2], (8, LANES))
                inv_ref[jj, g * 8 : (g + 1) * 8, p * LANES : (p + 1) * LANES] = 1.0 / (
                    jnp.where(low, even, odd) - cols
                )


def denominators(ti, slab, eps_occ, eps_vir, capt, across):
    return pl.pallas_call(
        functools.partial(denom_kernel, capt, across),
        in_specs=[SMEM, SMEM, SMEM, VMEM],
        out_specs=VMEM,
        scratch_shapes=[pltpu.VMEM((2 * capt, 64), F32)] * 2,
        out_shape=jax.ShapeDtypeStruct((2, capt, TILE * TILE), F32),
        cost_estimate=pl.CostEstimate(flops=10**7, bytes_accessed=10**6, transcendentals=0),
        name="denominators",
    )(ti, slab, eps_occ, eps_vir.reshape(across, 64))


def multiply_kernel(which, nq, nmax, unroll, meta_ref, tiles_ref, *refs):
    amps_refs, refs = refs[:nq], refs[nq:]
    if which == 0:
        sum_ref, amps_ref = refs
        sum_ref[...] = jnp.zeros(sum_ref.shape, F32)
    else:
        sum_ref, out_refs, amps_ref = refs[0], refs[1:-1], refs[-1]
    for q in range(nq):
        amps_ref[q * LIVE2 : (q + 1) * LIVE2] = amps_refs[q][...]
    low = lax.broadcasted_iota(jnp.int32, (ROWS, LANES), 1) < 64

    def spread(w):
        w = w.astype(F32)
        r = pltpu.roll(w, 64, 1)
        zero = jnp.zeros_like(w)
        parts = [
            jnp.where(low, w, zero),
            jnp.where(low, r, zero),
            jnp.where(low, zero, r),
            jnp.where(low, zero, w),
        ]
        return jnp.concatenate(parts, axis=0).astype(BF16)

    total = meta_ref[15 * nmax + which]

    def several(step, carry):
        results = []
        for u in range(unroll):
            e = jnp.minimum(step * unroll + u, total - 1)
            at = which * 5 * nmax + e
            left = jnp.concatenate(
                [amps_ref[meta_ref[nmax + at]], amps_ref[meta_ref[2 * nmax + at]]], axis=1
            )
            right = jnp.concatenate(
                [spread(tiles_ref[e, 0:ROWS]), spread(tiles_ref[e, ROWS : 2 * ROWS])], axis=0
            )
            place = jnp.where(step * unroll + u < total, meta_ref[at], nq * LIVE2)
            results.append((place, jnp.dot(left, right, preferred_element_type=F32)))
        for place, value in results:
            if which == 0:
                sum_ref[place] = value
            else:
                sum_ref[place] += value
        return carry

    lax.fori_loop(0, (total + unroll - 1) // unroll, several, 0)
    if which == 1:
        for q in range(nq):
            out_refs[q][...] = sum_ref[q * LIVE2 : (q + 1) * LIVE2].astype(BF16)


def multiply(which, meta, tiles, amps, sums, nq):
    block = jax.ShapeDtypeStruct((LIVE2, ROWS, LANES), BF16)
    total = jax.ShapeDtypeStruct((nq * LIVE2 + 1, ROWS, LANES), F32)
    out = [block] * nq if which == 1 else total
    return pl.pallas_call(
        functools.partial(multiply_kernel, which, nq, nq * LIVE2 + 8, 8),
        in_specs=[SMEM] + [VMEM] * (1 + len(amps) + len(sums)),
        out_specs=jax.tree.map(lambda _: VMEM, out),
        out_shape=out,
        scratch_shapes=[pltpu.VMEM((nq * LIVE2, ROWS, LANES), BF16)],
        compiler_params=pltpu.CompilerParams(vmem_limit_bytes=24 * 1024 * 1024),
        cost_estimate=pl.CostEstimate(flops=10**9, bytes_accessed=6 * 10**6, transcendentals=0),
        name=("multiply_own", "multiply_sibling")[which],
    )(meta, tiles, *amps, *sums)


def update_kernel(
    capt, across, nq, ti_ref, amps_ref, ovov_ref, hist_ref, inv_ref, *refs
):
    part_refs, (new_ref, gram_ref, sum_ref) = refs[:nq], refs[nq:]
    nhist = hist_ref.shape[0]
    first = lax.axis_index("pair")
    second = lax.axis_index("reorder") * 2

    def add(s, carry):
        acc = part_refs[0][s].astype(F32)
        for part_ref in part_refs[1:]:
            acc = acc + part_ref[s].astype(F32)
        sum_ref[pl.ds(pl.multiple_of(s * ROWS, ROWS), ROWS), :] = acc
        return carry

    lax.fori_loop(0, LIVE2, add, 0, unroll=4)
    slot = lax.broadcasted_iota(jnp.int32, (8, LANES), 0)
    accs = [jnp.zeros((8, LANES), F32) for _ in range(nhist + 1)]
    for jj in range(2):
        count = count_live(ti_ref, first, second + jj, capt, across * across)
        start = 0 if jj == 0 else (LIVE2 - count) * ROWS
        for g in range(capt // 8):
            alive = slot + g * 8 < count
            rows = slice(g * 8, (g + 1) * 8)

            def chunk(p, accs):
                here = pl.ds(pl.multiple_of(p * LANES, LANES), LANES)
                cycle = sum_ref[pl.ds(start + g * 8 * ROWS + p, 8, stride=ROWS), :]
                resid = jnp.where(alive, ovov_ref[0, jj, rows, here].astype(F32) + cycle, 0.0)
                moved = amps_ref[0, jj, rows, here].astype(F32) + resid * inv_ref[jj, rows, here]
                new_ref[0, jj, rows, here] = jnp.where(alive, moved, 0.0).astype(BF16)
                out = [
                    accs[m] + hist_ref[m, 0, jj, rows, here].astype(F32) * resid
                    for m in range(nhist)
                ]
                out.append(accs[nhist] + resid * resid)
                return out

            accs = lax.fori_loop(0, ROWS, chunk, accs, unroll=8)
    lane = lax.broadcasted_iota(jnp.int32, (1, LANES), 1)
    row = jnp.zeros((1, LANES), F32)
    for m in range(nhist + 1):
        row = jnp.where(lane == m, jnp.sum(accs[m]), row)
    for n in range(gram_ref.shape[0]):
        gram_ref[n] = row


def update(ti, amps, ovov, history, inv, parts, copies, capt, across):
    nq = len(parts)
    return pl.pallas_call(
        functools.partial(update_kernel, capt, across, nq),
        in_specs=[SMEM] + [VMEM] * (4 + nq),
        out_specs=[VMEM, VMEM],
        out_shape=[
            jax.ShapeDtypeStruct(amps.shape, BF16),
            jax.ShapeDtypeStruct((copies, 1, LANES), F32),
        ],
        scratch_shapes=[
            pltpu.VMEM(((LIVE2 + capt) * ROWS, LANES), F32),
        ],
        compiler_params=pltpu.CompilerParams(vmem_limit_bytes=24 * 1024 * 1024),
        cost_estimate=pl.CostEstimate(flops=10**8, bytes_accessed=6 * 10**6, transcendentals=0),
        name="update_amps",
    )(ti, amps, ovov, history, inv, *parts)


def finish_kernel(nhist, scale, sums_ref, out_ref):
    total = sums_ref[0]
    for n in range(1, sums_ref.shape[0]):
        total = total + sums_ref[n]
    lane = lax.broadcasted_iota(jnp.int32, total.shape, 1)
    total = jnp.where(lane == nhist, jnp.sqrt(jnp.maximum(total, 0.0)), total) * scale
    out_ref[...] = total[0, : nhist + 1]


def finish(sums, nhist, scale):
    return pl.pallas_call(
        functools.partial(finish_kernel, nhist, scale),
        in_specs=[VMEM],
        out_specs=VMEM,
        out_shape=jax.ShapeDtypeStruct((nhist + 1,), F32),
        name="finish_gram",
    )(sums)


def swap(x, axis, size, step):
    return lax.ppermute(x, axis, [(n, n ^ step) for n in range(size)])


def spread_perm(npair, nq, m):
    return [
        (z * npair + p, ((p // 2) ^ m) * npair + 2 * z + p % 2)
        for z in range(nq)
        for p in range(npair)
    ]


def local(npair, nq, amps, tile_index, ovov, cycle_ints, history, slab, eps_occ, eps_vir):
    occ_dev, jdev, capt, tile_area = amps.shape
    ns = tile_index.shape[0]
    across = cycle_ints.shape[2]
    nhist = history.shape[0]
    assert occ_dev == 1 and jdev == 2 and tile_area == TILE * TILE and capt == 16
    assert ns == npair == 2 * nq
    packed = pack(amps, tile_index, capt, across)
    axes = ("reorder", "pair")
    order = [n // 2 if n % 2 == 0 else nq - 1 - n // 2 for n in range(nq)]
    turned = [lax.ppermute(packed, axes, spread_perm(npair, nq, m)) for m in order]
    late = lax.optimization_barrier((packed, cycle_ints, tile_index, slab, eps_occ, eps_vir))
    meta, mine, send = prep(*late[1:3], capt, across, nq)
    inv = denominators(*late[2:], capt, across)
    turned, send, inv = lax.optimization_barrier((turned, send, inv))
    turned = [turned[order.index(m)] for m in range(nq)]
    theirs = swap(send, "pair", npair, 1)
    sums = multiply(0, meta, mine, turned, [], nq)
    partial = multiply(1, meta, theirs, turned, [sums], nq)
    parts = [partial[0]] + [swap(partial[e], "pair", npair, 2 * e) for e in range(1, nq)]
    new_amps, gram = update(
        tile_index, amps, ovov, history, inv, parts, npair * nq, capt, across
    )
    sums = lax.all_to_all(gram, axes, split_axis=0, concat_axis=0, tiled=True)
    return (new_amps, finish(sums, nhist, 1.0 / (TILE * ns)))


def solution(mesh):
    in_specs = (
        P("pair", "reorder", None, None),
        P(),
        P("pair", "reorder", None, None),
        P("pair", "reorder", None, None, None),
        P(None, "pair", "reorder", None, None),
        P(),
        P(),
        P(),
    )
    out_specs = (P("pair", "reorder", None, None), P())
    body = functools.partial(local, mesh.shape["pair"], mesh.shape["reorder"])
    return jax.shard_map(body, mesh=mesh, in_specs=in_specs, out_specs=out_specs, check_vma=False)
```

```python
import functools

import jax
import jax.numpy as jnp
from jax import lax
from jax.experimental import pallas as pl
from jax.experimental.pallas import tpu as pltpu
from jax.sharding import PartitionSpec as P

TILE = 64
ROWS = 32
LANES = 128
LIVE2 = 24
F32 = jnp.float32
BF16 = jnp.bfloat16
SMEM = pl.BlockSpec(memory_space=pltpu.SMEM)
VMEM = pl.BlockSpec(memory_space=pltpu.VMEM)


def count_live(ti_ref, i, j, capt, dead):
    total = jnp.int32(0)
    for s in range(capt):
        total = total + (ti_ref[i, j, s] < dead).astype(jnp.int32)
    return total


def row_of(idx, across):
    factor = -(-(1 << 17) // across)
    assert all((n * factor) >> 17 == n // across for n in range(across * across + 1))
    return lax.shift_right_logical(idx * factor, 17)


def pack_kernel(capt, across, ti_ref, amps_ref, out_ref, flat_ref, turned_ref):
    first = lax.axis_index("pair")
    second = lax.axis_index("reorder") * 2
    live1 = count_live(ti_ref, first, second + 1, capt, across * across)
    for jj in range(2):
        for p in range(ROWS):
            chunk = amps_ref[0, jj, :, p * LANES : (p + 1) * LANES].astype(F32)
            for g in range(capt // 8):
                start = (jj * capt + g * 8) * ROWS + p
                flat_ref[pl.ds(start, 8, stride=ROWS), :] = chunk[g * 8 : (g + 1) * 8]
    old = lax.broadcasted_iota(jnp.int32, (LANES, LANES), 0)
    new = lax.broadcasted_iota(jnp.int32, (LANES, LANES), 1)
    source = (new // 64) * 64 + (new % 32) * 2 + (new % 64) // 32
    turn = (old == source).astype(F32).astype(BF16)
    turned_ref[...] = jnp.dot(
        flat_ref[...].astype(BF16), turn, preferred_element_type=F32
    ).astype(BF16)
    out_ref[0:capt] = turned_ref[0 : capt * ROWS].reshape(capt, ROWS, LANES)
    out_ref[capt:LIVE2] = jnp.zeros((LIVE2 - capt, ROWS, LANES), BF16)

    def place(s, carry):
        start = pl.multiple_of((capt + s) * ROWS, ROWS)
        out_ref[LIVE2 - live1 + s] = turned_ref[pl.ds(start, ROWS), :]
        return carry

    lax.fori_loop(0, live1, place, 0)


def pack(amps, ti, capt, across):
    return pl.pallas_call(
        functools.partial(pack_kernel, capt, across),
        in_specs=[SMEM, VMEM],
        out_specs=VMEM,
        scratch_shapes=[
            pltpu.VMEM((2 * capt * ROWS, LANES), F32),
            pltpu.VMEM((2 * capt * ROWS, LANES), BF16),
        ],
        out_shape=jax.ShapeDtypeStruct((LIVE2, ROWS, LANES), BF16),
        cost_estimate=pl.CostEstimate(flops=10**8, bytes_accessed=500000, transcendentals=0),
        name="pack_amps",
    )(ti, amps)


def prep_kernel(
    capt, across, nq, nmax, ti_ref, hbm_ref,
    meta_ref, mine_ref, send0_ref, send1_ref, ints_ref, wide_ref, tab_ref, sem,
):
    stride = nmax + 8
    fetch_ints = pltpu.make_async_copy(hbm_ref, ints_ref, sem)
    fetch_ints.start()
    dead = across * across
    me = lax.axis_index("pair")
    sibling = me ^ 1
    plane = lax.axis_index("reorder")
    second = plane * 2

    def build(which, who, k):
        def field(f):
            return (which * 5 + f) * stride

        parity = lax.rem(k, 2)

        def one_first(n, cnt):
            e = jnp.where(n < nq // 2, nq, 2 * nq - 1) - 1 - 2 * n
            i = who ^ (2 * e)
            q = lax.shift_right_logical(who, 1) ^ plane ^ e
            out = n * LIVE2
            for a in range(across + 1):
                tab_ref[a] = -1
            live_in = jnp.int32(0)
            for t in range(capt):
                idx = ti_ref[i, k, t]
                live_in = live_in + (idx < dead).astype(jnp.int32)
                a = row_of(idx, across)
                held = t * 32 + idx - a * across
                old = tab_ref[a]
                tab_ref[a] = jnp.where(old < 0, held, old)
                tab_ref[32 + a] = jnp.where(old < 0, -1, held)
            shift = q * LIVE2 + jnp.where(parity == 1, LIVE2 - live_in, 0)
            live1 = count_live(ti_ref, i, second + 1, capt, dead)
            for jj in range(2):
                for s in range(capt):
                    idx = ti_ref[i, second + jj, s]
                    a = row_of(idx, across)
                    b = idx - a * across
                    h0 = tab_ref[a]
                    h1 = tab_ref[32 + a]
                    hit = (idx < dead) & (h0 >= 0)
                    both = h1 >= 0
                    if which < 2:
                        place = out + (s if jj == 0 else LIVE2 - live1 + s)
                        meta_ref[field(0) + cnt] = place
                        t0 = shift + lax.shift_right_arithmetic(h0, 5)
                        t1 = shift + lax.shift_right_arithmetic(h1, 5)
                        meta_ref[field(1) + cnt] = t0
                        meta_ref[field(2) + cnt] = jnp.where(both, t1, t0)
                    if which != 1:
                        w0 = ((h0 & 31) * across + b) * 2 + jj
                        w1 = ((h1 & 31) * across + b) * 2 + jj
                        meta_ref[field(3) + cnt] = w0
                        meta_ref[field(4) + cnt] = jnp.where(both, w1, -1)
                    cnt = cnt + hit.astype(jnp.int32)
            return cnt

        for group in range(2):
            end = lax.fori_loop(
                group * nq // 2, (group + 1) * nq // 2, one_first, jnp.int32(group * nmax // 2)
            )
            meta_ref[15 * stride + 2 * which + group] = end

    def gather(which, group, tiles_ref, offset):
        first = group * nmax // 2
        total = meta_ref[15 * stride + 2 * which + group]

        def fetch(step, carry):
            for u in range(4):
                e = jnp.minimum(first + step * 4 + u, total - 1)
                for m in range(2):
                    at = jnp.maximum(meta_ref[(which * 5 + 3 + m) * stride + e], 0)
                    wide_ref[2 * u + m] = ints_ref[lax.shift_right_logical(at, 1)].astype(F32)
            for u in range(4):
                e = jnp.minimum(first + step * 4 + u, total - 1)
                for m in range(2):
                    at = meta_ref[(which * 5 + 3 + m) * stride + e]
                    jj = jnp.maximum(at, 0) & 1
                    tile = wide_ref[2 * u + m, pl.ds(jj, ROWS, stride=2), :]
                    if m == 1:
                        tile = jnp.where(at >= 0, tile, 0.0)
                    tiles_ref[e - offset, m * ROWS : (m + 1) * ROWS] = tile.astype(BF16)
            return carry

        lax.fori_loop(0, (total - first + 3) // 4, fetch, 0)

    build(2, sibling, me)
    build(0, me, me)
    build(1, me, sibling)
    fetch_ints.wait()
    for group, send_ref in enumerate((send0_ref, send1_ref)):
        gather(2, group, send_ref, group * nmax // 2)
    for group in range(2):
        gather(0, group, mine_ref, 0)


def prep(cycle_ints, ti, capt, across, nq):
    nmax = nq * LIVE2
    ints = cycle_ints[0].transpose(1, 2, 0, 3).reshape(across, across, 2, ROWS, LANES)
    ints = ints.transpose(0, 1, 3, 2, 4).reshape(across * across, 2 * ROWS, LANES)
    tiles = jax.ShapeDtypeStruct((nmax, 2 * ROWS, LANES), BF16)
    half = jax.ShapeDtypeStruct((nmax // 2, 2 * ROWS, LANES), BF16)
    return pl.pallas_call(
        functools.partial(prep_kernel, capt, across, nq, nmax),
        in_specs=[SMEM, pl.BlockSpec(memory_space=pltpu.HBM)],
        out_specs=[SMEM, VMEM, VMEM, VMEM],
        scratch_shapes=[
            pltpu.VMEM(ints.shape, BF16),
            pltpu.VMEM((8, 2 * ROWS, LANES), F32),
            pltpu.SMEM((64,), jnp.int32),
            pltpu.SemaphoreType.DMA,
        ],
        out_shape=[
            jax.ShapeDtypeStruct((15 * (nmax + 8) + 8,), jnp.int32), tiles, half, half
        ],
        compiler_params=pltpu.CompilerParams(vmem_limit_bytes=50 * 1024 * 1024),
        cost_estimate=pl.CostEstimate(flops=10**9, bytes_accessed=40 * 10**6, transcendentals=0),
        name="prep_integrals",
    )(ti, ints)


def denom_kernel(capt, across, ti_ref, slab_ref, occ_ref, vir_ref, inv_ref, row_ref, col_ref):
    first = lax.axis_index("pair")
    second = lax.axis_index("reorder") * 2
    occ_i = occ_ref[slab_ref[first]]
    low = lax.broadcasted_iota(jnp.int32, (8, LANES), 1) < 64
    for jj in range(2):
        for s in range(capt):
            idx = ti_ref[first, second + jj, s]
            row = row_of(idx, across)
            a = jnp.minimum(row, across - 1)
            b = idx - row * across
            row_ref[jj * capt + s] = vir_ref[a]
            col_ref[jj * capt + s] = vir_ref[b]
    for jj in range(2):
        occ = occ_i + occ_ref[slab_ref[second + jj]]
        for g in range(capt // 8):
            here = pl.ds(jj * capt + g * 8, 8)
            rows = occ - row_ref[here]
            col = col_ref[here]
            cols = jnp.concatenate([col, col], axis=1)
            for p in range(ROWS):
                even = jnp.broadcast_to(rows[:, 2 * p : 2 * p + 1], (8, LANES))
                odd = jnp.broadcast_to(rows[:, 2 * p + 1 : 2 * p + 2], (8, LANES))
                inv_ref[jj, g * 8 : (g + 1) * 8, p * LANES : (p + 1) * LANES] = 1.0 / (
                    jnp.where(low, even, odd) - cols
                )


def denominators(ti, slab, eps_occ, eps_vir, capt, across):
    return pl.pallas_call(
        functools.partial(denom_kernel, capt, across),
        in_specs=[SMEM, SMEM, SMEM, VMEM],
        out_specs=VMEM,
        scratch_shapes=[pltpu.VMEM((2 * capt, 64), F32)] * 2,
        out_shape=jax.ShapeDtypeStruct((2, capt, TILE * TILE), F32),
        cost_estimate=pl.CostEstimate(flops=10**7, bytes_accessed=10**6, transcendentals=0),
        name="denominators",
    )(ti, slab, eps_occ, eps_vir.reshape(across, 64))


def sum_order(nq):
    return [e for e in range(nq - 1, -1, -2)] + [e for e in range(nq - 2, -1, -2)]


def multiply_kernel(group, nq, nmax, unroll, meta_ref, tiles_ref, *refs):
    amps_refs, refs = refs[:nq], refs[nq:]
    half = nmax // 2
    stride = nmax + 8
    if group is None:
        sum_ref, amps_ref = refs
        sum_ref[...] = jnp.zeros(sum_ref.shape, F32)
    else:
        own_ref, out_refs, (amps_ref, sum_ref) = refs[0], refs[1:-2], refs[-2:]
        sum_ref[0:half] = own_ref[group * half : (group + 1) * half]
    for q in range(nq):
        amps_ref[q * LIVE2 : (q + 1) * LIVE2] = amps_refs[q][...]
    low = lax.broadcasted_iota(jnp.int32, (ROWS, LANES), 1) < 64

    def spread(w):
        w = w.astype(F32)
        r = pltpu.roll(w, 64, 1)
        zero = jnp.zeros_like(w)
        parts = [
            jnp.where(low, w, zero),
            jnp.where(low, r, zero),
            jnp.where(low, zero, r),
            jnp.where(low, zero, w),
        ]
        return jnp.concatenate(parts, axis=0).astype(BF16)

    for g in range(2) if group is None else [group]:
        which = 0 if group is None else 1
        first = g * half
        total = meta_ref[15 * stride + 2 * which + g]

        def several(step, carry):
            results = []
            for u in range(unroll):
                e = jnp.minimum(first + step * unroll + u, total - 1)
                at = which * 5 * stride + e
                left = jnp.concatenate(
                    [amps_ref[meta_ref[stride + at]], amps_ref[meta_ref[2 * stride + at]]],
                    axis=1,
                )
                tile = e if group is None else e - first
                right = jnp.concatenate(
                    [
                        spread(tiles_ref[tile, 0:ROWS]),
                        spread(tiles_ref[tile, ROWS : 2 * ROWS]),
                    ],
                    axis=0,
                )
                place = meta_ref[at]
                if group is not None:
                    inside = first + step * unroll + u < total
                    place = jnp.where(inside, place - first, half)
                results.append((place, jnp.dot(left, right, preferred_element_type=F32)))
            for place, value in results:
                if group is None:
                    sum_ref[place] = value
                else:
                    sum_ref[place] += value
            return carry

        lax.fori_loop(0, (total - first + unroll - 1) // unroll, several, 0)
    if group is not None:
        for n in range(nq // 2):
            out_refs[n][...] = sum_ref[n * LIVE2 : (n + 1) * LIVE2].astype(BF16)


def multiply(group, meta, tiles, amps, sums, nq):
    nmax = nq * LIVE2
    scratch = [pltpu.VMEM((nmax, ROWS, LANES), BF16)]
    if group is None:
        out = jax.ShapeDtypeStruct((nmax, ROWS, LANES), F32)
    else:
        out = [jax.ShapeDtypeStruct((LIVE2, ROWS, LANES), BF16)] * (nq // 2)
        scratch.append(pltpu.VMEM((nmax // 2 + 1, ROWS, LANES), F32))
    return pl.pallas_call(
        functools.partial(multiply_kernel, group, nq, nmax, 8),
        in_specs=[SMEM] + [VMEM] * (1 + len(amps) + len(sums)),
        out_specs=jax.tree.map(lambda _: VMEM, out),
        out_shape=out,
        scratch_shapes=scratch,
        compiler_params=pltpu.CompilerParams(vmem_limit_bytes=24 * 1024 * 1024),
        cost_estimate=pl.CostEstimate(flops=10**9, bytes_accessed=6 * 10**6, transcendentals=0),
        name="multiply_own" if group is None else f"multiply_sibling_{group}",
    )(meta, tiles, *amps, *sums)


def update_kernel(
    capt, across, nq, ti_ref, amps_ref, ovov_ref, hist_ref, inv_ref, *refs
):
    part_refs, (new_ref, gram_ref, sum_ref) = refs[:nq], refs[nq:]
    nhist = hist_ref.shape[0]
    first = lax.axis_index("pair")
    second = lax.axis_index("reorder") * 2

    def add(s, carry):
        acc = part_refs[0][s].astype(F32)
        for part_ref in part_refs[1:]:
            acc = acc + part_ref[s].astype(F32)
        sum_ref[pl.ds(pl.multiple_of(s * ROWS, ROWS), ROWS), :] = acc
        return carry

    lax.fori_loop(0, LIVE2, add, 0, unroll=4)
    slot = lax.broadcasted_iota(jnp.int32, (8, LANES), 0)
    accs = [jnp.zeros((8, LANES), F32) for _ in range(nhist + 1)]
    for jj in range(2):
        count = count_live(ti_ref, first, second + jj, capt, across * across)
        start = 0 if jj == 0 else (LIVE2 - count) * ROWS
        for g in range(capt // 8):
            alive = slot + g * 8 < count
            rows = slice(g * 8, (g + 1) * 8)

            def chunk(p, accs):
                here = pl.ds(pl.multiple_of(p * LANES, LANES), LANES)
                cycle = sum_ref[pl.ds(start + g * 8 * ROWS + p, 8, stride=ROWS), :]
                resid = jnp.where(alive, ovov_ref[0, jj, rows, here].astype(F32) + cycle, 0.0)
                moved = amps_ref[0, jj, rows, here].astype(F32) + resid * inv_ref[jj, rows, here]
                new_ref[0, jj, rows, here] = jnp.where(alive, moved, 0.0).astype(BF16)
                out = [
                    accs[m] + hist_ref[m, 0, jj, rows, here].astype(F32) * resid
                    for m in range(nhist)
                ]
                out.append(accs[nhist] + resid * resid)
                return out

            accs = lax.fori_loop(0, ROWS, chunk, accs, unroll=8)
    lane = lax.broadcasted_iota(jnp.int32, (1, LANES), 1)
    row = jnp.zeros((1, LANES), F32)
    for m in range(nhist + 1):
        row = jnp.where(lane == m, jnp.sum(accs[m]), row)
    for n in range(gram_ref.shape[0]):
        gram_ref[n] = row


def update(ti, amps, ovov, history, inv, parts, copies, capt, across):
    nq = len(parts)
    return pl.pallas_call(
        functools.partial(update_kernel, capt, across, nq),
        in_specs=[SMEM] + [VMEM] * (4 + nq),
        out_specs=[VMEM, VMEM],
        out_shape=[
            jax.ShapeDtypeStruct(amps.shape, BF16),
            jax.ShapeDtypeStruct((copies, 1, LANES), F32),
        ],
        scratch_shapes=[
            pltpu.VMEM(((LIVE2 + capt) * ROWS, LANES), F32),
        ],
        compiler_params=pltpu.CompilerParams(vmem_limit_bytes=24 * 1024 * 1024),
        cost_estimate=pl.CostEstimate(flops=10**8, bytes_accessed=6 * 10**6, transcendentals=0),
        name="update_amps",
    )(ti, amps, ovov, history, inv, *parts)


def finish_kernel(nhist, scale, sums_ref, out_ref):
    total = sums_ref[0]
    for n in range(1, sums_ref.shape[0]):
        total = total + sums_ref[n]
    lane = lax.broadcasted_iota(jnp.int32, total.shape, 1)
    total = jnp.where(lane == nhist, jnp.sqrt(jnp.maximum(total, 0.0)), total) * scale
    out_ref[...] = total[0, : nhist + 1]


def finish(sums, nhist, scale):
    return pl.pallas_call(
        functools.partial(finish_kernel, nhist, scale),
        in_specs=[VMEM],
        out_specs=VMEM,
        out_shape=jax.ShapeDtypeStruct((nhist + 1,), F32),
        name="finish_gram",
    )(sums)


def swap(x, axis, size, step):
    return lax.ppermute(x, axis, [(n, n ^ step) for n in range(size)])


def spread_perm(npair, nq, m):
    return [
        (z * npair + p, ((p // 2) ^ m) * npair + 2 * z + p % 2)
        for z in range(nq)
        for p in range(npair)
    ]


def local(npair, nq, amps, tile_index, ovov, cycle_ints, history, slab, eps_occ, eps_vir):
    occ_dev, jdev, capt, tile_area = amps.shape
    ns = tile_index.shape[0]
    across = cycle_ints.shape[2]
    nhist = history.shape[0]
    assert occ_dev == 1 and jdev == 2 and tile_area == TILE * TILE and capt == 16
    assert ns == npair == 2 * nq
    packed = pack(amps, tile_index, capt, across)
    axes = ("reorder", "pair")
    order = [n // 2 if n % 2 == 0 else nq - 1 - n // 2 for n in range(nq)][::-1]
    turned = [lax.ppermute(packed, axes, spread_perm(npair, nq, m)) for m in order]
    late = lax.optimization_barrier((packed, cycle_ints, tile_index, slab, eps_occ, eps_vir))
    meta, mine, *send = prep(*late[1:3], capt, across, nq)
    inv = denominators(*late[2:], capt, across)
    turned, send, inv = lax.optimization_barrier((turned, send, inv))
    turned = [turned[order.index(m)] for m in range(nq)]
    theirs = [swap(tiles, "pair", npair, 1) for tiles in send]
    sums = multiply(None, meta, mine, turned, [], nq)
    partial = []
    for group in range(2):
        partial += multiply(group, meta, theirs[group], turned, [sums], nq)
    parts = [
        swap(part, "pair", npair, 2 * e) if e else part
        for e, part in zip(sum_order(nq), partial)
    ]
    new_amps, gram = update(
        tile_index, amps, ovov, history, inv, parts, npair * nq, capt, across
    )
    sums = lax.all_to_all(gram, axes, split_axis=0, concat_axis=0, tiled=True)
    return (new_amps, finish(sums, nhist, 1.0 / (TILE * ns)))


def solution(mesh):
    in_specs = (
        P("pair", "reorder", None, None),
        P(),
        P("pair", "reorder", None, None),
        P("pair", "reorder", None, None, None),
        P(None, "pair", "reorder", None, None),
        P(),
        P(),
        P(),
    )
    out_specs = (P("pair", "reorder", None, None), P())
    body = functools.partial(local, mesh.shape["pair"], mesh.shape["reorder"])
    return jax.shard_map(body, mesh=mesh, in_specs=in_specs, out_specs=out_specs, check_vma=False)
```

```python
import functools

import jax
import jax.numpy as jnp
from jax import lax
from jax.experimental import pallas as pl
from jax.experimental.pallas import tpu as pltpu
from jax.sharding import PartitionSpec as P

TILE = 64
ROWS = 32
LANES = 128
LIVE2 = 24
F32 = jnp.float32
BF16 = jnp.bfloat16
SMEM = pl.BlockSpec(memory_space=pltpu.SMEM)
VMEM = pl.BlockSpec(memory_space=pltpu.VMEM)


def count_live(ti_ref, i, j, capt, dead):
    total = jnp.int32(0)
    for s in range(capt):
        total = total + (ti_ref[i, j, s] < dead).astype(jnp.int32)
    return total


def row_of(idx, across):
    factor = -(-(1 << 17) // across)
    assert all((n * factor) >> 17 == n // across for n in range(across * across + 1))
    return lax.shift_right_logical(idx * factor, 17)


def pack_kernel(capt, across, ti_ref, amps_ref, out_ref, flat_ref, turned_ref):
    first = lax.axis_index("pair")
    second = lax.axis_index("reorder") * 2
    live1 = count_live(ti_ref, first, second + 1, capt, across * across)
    for jj in range(2):
        for p in range(ROWS):
            chunk = amps_ref[0, jj, :, p * LANES : (p + 1) * LANES].astype(F32)
            for g in range(capt // 8):
                start = (jj * capt + g * 8) * ROWS + p
                flat_ref[pl.ds(start, 8, stride=ROWS), :] = chunk[g * 8 : (g + 1) * 8]
    old = lax.broadcasted_iota(jnp.int32, (LANES, LANES), 0)
    new = lax.broadcasted_iota(jnp.int32, (LANES, LANES), 1)
    source = (new // 64) * 64 + (new % 32) * 2 + (new % 64) // 32
    turn = (old == source).astype(F32).astype(BF16)
    turned_ref[...] = jnp.dot(
        flat_ref[...].astype(BF16), turn, preferred_element_type=F32
    ).astype(BF16)
    out_ref[0:capt] = turned_ref[0 : capt * ROWS].reshape(capt, ROWS, LANES)
    out_ref[capt:LIVE2] = jnp.zeros((LIVE2 - capt, ROWS, LANES), BF16)

    def place(s, carry):
        start = pl.multiple_of((capt + s) * ROWS, ROWS)
        out_ref[LIVE2 - live1 + s] = turned_ref[pl.ds(start, ROWS), :]
        return carry

    lax.fori_loop(0, live1, place, 0)


def pack(amps, ti, capt, across):
    return pl.pallas_call(
        functools.partial(pack_kernel, capt, across),
        in_specs=[SMEM, VMEM],
        out_specs=VMEM,
        scratch_shapes=[
            pltpu.VMEM((2 * capt * ROWS, LANES), F32),
            pltpu.VMEM((2 * capt * ROWS, LANES), BF16),
        ],
        out_shape=jax.ShapeDtypeStruct((LIVE2, ROWS, LANES), BF16),
        cost_estimate=pl.CostEstimate(flops=10**8, bytes_accessed=500000, transcendentals=0),
        name="pack_amps",
    )(ti, amps)


def prep_kernel(
    capt, across, nq, nmax, ti_ref, hbm_ref,
    meta_ref, mine_ref, send0_ref, send1_ref, ints_ref, wide_ref, tab_ref, sem,
):
    stride = nmax + 8
    fetch_ints = pltpu.make_async_copy(hbm_ref, ints_ref, sem)
    fetch_ints.start()
    dead = across * across
    me = lax.axis_index("pair")
    sibling = me ^ 1
    plane = lax.axis_index("reorder")
    second = plane * 2

    def build(which, who, k):
        def field(f):
            return (which * 5 + f) * stride

        parity = lax.rem(k, 2)

        def one_first(n, cnt):
            e = jnp.where(n < nq // 2, nq, 2 * nq - 1) - 1 - 2 * n
            i = who ^ (2 * e)
            q = lax.shift_right_logical(who, 1) ^ plane ^ e
            out = n * LIVE2
            for a in range(across + 1):
                tab_ref[a] = -1
            live_in = jnp.int32(0)
            for t in range(capt):
                idx = ti_ref[i, k, t]
                live_in = live_in + (idx < dead).astype(jnp.int32)
                a = row_of(idx, across)
                held = t * 32 + idx - a * across
                old = tab_ref[a]
                tab_ref[a] = jnp.where(old < 0, held, old)
                tab_ref[32 + a] = jnp.where(old < 0, -1, held)
            shift = q * LIVE2 + jnp.where(parity == 1, LIVE2 - live_in, 0)
            live1 = count_live(ti_ref, i, second + 1, capt, dead)
            for jj in range(2):
                for s in range(capt):
                    idx = ti_ref[i, second + jj, s]
                    a = row_of(idx, across)
                    b = idx - a * across
                    h0 = tab_ref[a]
                    h1 = tab_ref[32 + a]
                    hit = (idx < dead) & (h0 >= 0)
                    both = h1 >= 0
                    if which < 2:
                        place = out + (s if jj == 0 else LIVE2 - live1 + s)
                        meta_ref[field(0) + cnt] = place
                        t0 = shift + lax.shift_right_arithmetic(h0, 5)
                        t1 = shift + lax.shift_right_arithmetic(h1, 5)
                        meta_ref[field(1) + cnt] = t0
                        meta_ref[field(2) + cnt] = jnp.where(both, t1, t0)
                    if which != 1:
                        w0 = ((h0 & 31) * across + b) * 2 + jj
                        w1 = ((h1 & 31) * across + b) * 2 + jj
                        meta_ref[field(3) + cnt] = w0
                        meta_ref[field(4) + cnt] = jnp.where(both, w1, -1)
                    cnt = cnt + hit.astype(jnp.int32)
            return cnt

        for group in range(2):
            end = lax.fori_loop(
                group * nq // 2, (group + 1) * nq // 2, one_first, jnp.int32(group * nmax // 2)
            )
            meta_ref[15 * stride + 2 * which + group] = end

    def gather(which, group, tiles_ref, offset):
        first = group * nmax // 2
        total = meta_ref[15 * stride + 2 * which + group]

        def fetch(step, carry):
            for u in range(4):
                e = jnp.minimum(first + step * 4 + u, total - 1)
                for m in range(2):
                    at = jnp.maximum(meta_ref[(which * 5 + 3 + m) * stride + e], 0)
                    wide_ref[2 * u + m] = ints_ref[lax.shift_right_logical(at, 1)].astype(F32)
            for u in range(4):
                e = jnp.minimum(first + step * 4 + u, total - 1)
                for m in range(2):
                    at = meta_ref[(which * 5 + 3 + m) * stride + e]
                    jj = jnp.maximum(at, 0) & 1
                    tile = wide_ref[2 * u + m, pl.ds(jj, ROWS, stride=2), :]
                    if m == 1:
                        tile = jnp.where(at >= 0, tile, 0.0)
                    tiles_ref[e - offset, m * ROWS : (m + 1) * ROWS] = tile.astype(BF16)
            return carry

        lax.fori_loop(0, (total - first + 3) // 4, fetch, 0)

    build(2, sibling, me)
    build(0, me, me)
    build(1, me, sibling)
    fetch_ints.wait()
    for group, send_ref in enumerate((send0_ref, send1_ref)):
        gather(2, group, send_ref, group * nmax // 2)
    for group in range(2):
        gather(0, group, mine_ref, 0)


def prep(cycle_ints, ti, capt, across, nq):
    nmax = nq * LIVE2
    ints = cycle_ints[0].transpose(1, 2, 0, 3).reshape(across, across, 2, ROWS, LANES)
    ints = ints.transpose(0, 1, 3, 2, 4).reshape(across * across, 2 * ROWS, LANES)
    tiles = jax.ShapeDtypeStruct((nmax, 2 * ROWS, LANES), BF16)
    half = jax.ShapeDtypeStruct((nmax // 2, 2 * ROWS, LANES), BF16)
    return pl.pallas_call(
        functools.partial(prep_kernel, capt, across, nq, nmax),
        in_specs=[SMEM, pl.BlockSpec(memory_space=pltpu.HBM)],
        out_specs=[SMEM, VMEM, VMEM, VMEM],
        scratch_shapes=[
            pltpu.VMEM(ints.shape, BF16),
            pltpu.VMEM((8, 2 * ROWS, LANES), F32),
            pltpu.SMEM((64,), jnp.int32),
            pltpu.SemaphoreType.DMA,
        ],
        out_shape=[
            jax.ShapeDtypeStruct((15 * (nmax + 8) + 8,), jnp.int32), tiles, half, half
        ],
        compiler_params=pltpu.CompilerParams(vmem_limit_bytes=50 * 1024 * 1024),
        cost_estimate=pl.CostEstimate(flops=10**9, bytes_accessed=40 * 10**6, transcendentals=0),
        name="prep_integrals",
    )(ti, ints)


def denom_kernel(capt, across, ti_ref, slab_ref, occ_ref, vir_ref, inv_ref, row_ref, col_ref):
    first = lax.axis_index("pair")
    second = lax.axis_index("reorder") * 2
    occ_i = occ_ref[slab_ref[first]]
    low = lax.broadcasted_iota(jnp.int32, (8, LANES), 1) < 64
    for jj in range(2):
        for s in range(capt):
            idx = ti_ref[first, second + jj, s]
            row = row_of(idx, across)
            a = jnp.minimum(row, across - 1)
            b = idx - row * across
            row_ref[jj * capt + s] = vir_ref[a]
            col_ref[jj * capt + s] = vir_ref[b]
    for jj in range(2):
        occ = occ_i + occ_ref[slab_ref[second + jj]]
        for g in range(capt // 8):
            here = pl.ds(jj * capt + g * 8, 8)
            rows = occ - row_ref[here]
            col = col_ref[here]
            cols = jnp.concatenate([col, col], axis=1)
            for p in range(ROWS):
                even = jnp.broadcast_to(rows[:, 2 * p : 2 * p + 1], (8, LANES))
                odd = jnp.broadcast_to(rows[:, 2 * p + 1 : 2 * p + 2], (8, LANES))
                inv_ref[jj, g * 8 : (g + 1) * 8, p * LANES : (p + 1) * LANES] = 1.0 / (
                    jnp.where(low, even, odd) - cols
                )


def denominators(ti, slab, eps_occ, eps_vir, capt, across):
    return pl.pallas_call(
        functools.partial(denom_kernel, capt, across),
        in_specs=[SMEM, SMEM, SMEM, VMEM],
        out_specs=VMEM,
        scratch_shapes=[pltpu.VMEM((2 * capt, 64), F32)] * 2,
        out_shape=jax.ShapeDtypeStruct((2, capt, TILE * TILE), F32),
        cost_estimate=pl.CostEstimate(flops=10**7, bytes_accessed=10**6, transcendentals=0),
        name="denominators",
    )(ti, slab, eps_occ, eps_vir.reshape(across, 64))


def sum_order(nq):
    return [e for e in range(nq - 1, -1, -2)] + [e for e in range(nq - 2, -1, -2)]


def multiply_kernel(part, nq, nmax, unroll, meta_ref, *refs):
    half = nmax // 2
    stride = nmax + 8
    group = 1 if part == "both" else 0
    tiles = {"own": 1, "sibling": 1, "both": 2}[part]
    tiles_refs, amps_refs, refs = refs[:tiles], refs[tiles : tiles + nq], refs[tiles + nq :]
    if part == "own":
        sum_ref, amps_ref = refs
        work = [(0, tiles_refs[0], 0)]
    elif part == "sibling":
        own_ref, out_refs, (amps_ref, sum_ref) = refs[0], refs[1:-2], refs[-2:]
        work = [(1, tiles_refs[0], 0)]
    else:
        out_refs, (amps_ref, sum_ref) = refs[:-2], refs[-2:]
        work = [(0, tiles_refs[0], 0), (1, tiles_refs[1], half)]
    if part == "sibling":
        sum_ref[0:half] = own_ref[0:half]
    else:
        sum_ref[...] = jnp.zeros(sum_ref.shape, F32)
    for q in range(nq):
        amps_ref[q * LIVE2 : (q + 1) * LIVE2] = amps_refs[q][...]
    low = lax.broadcasted_iota(jnp.int32, (ROWS, LANES), 1) < 64

    def spread(w):
        w = w.astype(F32)
        r = pltpu.roll(w, 64, 1)
        zero = jnp.zeros_like(w)
        parts = [
            jnp.where(low, w, zero),
            jnp.where(low, r, zero),
            jnp.where(low, zero, r),
            jnp.where(low, zero, w),
        ]
        return jnp.concatenate(parts, axis=0).astype(BF16)

    first = group * half
    for which, tiles_ref, offset in work:
        total = meta_ref[15 * stride + 2 * which + group]

        def several(step, carry):
            results = []
            for u in range(unroll):
                e = jnp.minimum(first + step * unroll + u, total - 1)
                at = which * 5 * stride + e
                left = jnp.concatenate(
                    [amps_ref[meta_ref[stride + at]], amps_ref[meta_ref[2 * stride + at]]],
                    axis=1,
                )
                right = jnp.concatenate(
                    [
                        spread(tiles_ref[e - offset, 0:ROWS]),
                        spread(tiles_ref[e - offset, ROWS : 2 * ROWS]),
                    ],
                    axis=0,
                )
                inside = first + step * unroll + u < total
                place = jnp.where(inside, meta_ref[at] - first, half)
                results.append((place, jnp.dot(left, right, preferred_element_type=F32)))
            for place, value in results:
                if which == 0:
                    sum_ref[place] = value
                else:
                    sum_ref[place] += value
            return carry

        lax.fori_loop(0, (total - first + unroll - 1) // unroll, several, 0)
    if part != "own":
        for n in range(nq // 2):
            out_refs[n][...] = sum_ref[n * LIVE2 : (n + 1) * LIVE2].astype(BF16)


def multiply(part, meta, tiles, amps, sums, nq):
    nmax = nq * LIVE2
    scratch = [pltpu.VMEM((nmax, ROWS, LANES), BF16)]
    sum_shape = (nmax // 2 + 1, ROWS, LANES)
    if part == "own":
        out = jax.ShapeDtypeStruct(sum_shape, F32)
    else:
        out = [jax.ShapeDtypeStruct((LIVE2, ROWS, LANES), BF16)] * (nq // 2)
        scratch.append(pltpu.VMEM(sum_shape, F32))
    return pl.pallas_call(
        functools.partial(multiply_kernel, part, nq, nmax, 8),
        in_specs=[SMEM] + [VMEM] * (len(tiles) + len(amps) + len(sums)),
        out_specs=jax.tree.map(lambda _: VMEM, out),
        out_shape=out,
        scratch_shapes=scratch,
        compiler_params=pltpu.CompilerParams(vmem_limit_bytes=24 * 1024 * 1024),
        cost_estimate=pl.CostEstimate(flops=10**9, bytes_accessed=6 * 10**6, transcendentals=0),
        name="multiply_" + part,
    )(meta, *tiles, *amps, *sums)


def update_kernel(
    capt, across, nq, ti_ref, amps_ref, ovov_ref, hist_ref, inv_ref, *refs
):
    part_refs, (new_ref, gram_ref, sum_ref) = refs[:nq], refs[nq:]
    nhist = hist_ref.shape[0]
    first = lax.axis_index("pair")
    second = lax.axis_index("reorder") * 2

    def add(s, carry):
        acc = part_refs[0][s].astype(F32)
        for part_ref in part_refs[1:]:
            acc = acc + part_ref[s].astype(F32)
        sum_ref[pl.ds(pl.multiple_of(s * ROWS, ROWS), ROWS), :] = acc
        return carry

    lax.fori_loop(0, LIVE2, add, 0, unroll=4)
    slot = lax.broadcasted_iota(jnp.int32, (8, LANES), 0)
    accs = [jnp.zeros((8, LANES), F32) for _ in range(nhist + 1)]
    for jj in range(2):
        count = count_live(ti_ref, first, second + jj, capt, across * across)
        start = 0 if jj == 0 else (LIVE2 - count) * ROWS
        for g in range(capt // 8):
            alive = slot + g * 8 < count
            rows = slice(g * 8, (g + 1) * 8)

            def chunk(p, accs):
                here = pl.ds(pl.multiple_of(p * LANES, LANES), LANES)
                cycle = sum_ref[pl.ds(start + g * 8 * ROWS + p, 8, stride=ROWS), :]
                resid = jnp.where(alive, ovov_ref[0, jj, rows, here].astype(F32) + cycle, 0.0)
                moved = amps_ref[0, jj, rows, here].astype(F32) + resid * inv_ref[jj, rows, here]
                new_ref[0, jj, rows, here] = jnp.where(alive, moved, 0.0).astype(BF16)
                out = [
                    accs[m] + hist_ref[m, 0, jj, rows, here].astype(F32) * resid
                    for m in range(nhist)
                ]
                out.append(accs[nhist] + resid * resid)
                return out

            accs = lax.fori_loop(0, ROWS, chunk, accs, unroll=8)
    lane = lax.broadcasted_iota(jnp.int32, (1, LANES), 1)
    row = jnp.zeros((1, LANES), F32)
    for m in range(nhist + 1):
        row = jnp.where(lane == m, jnp.sum(accs[m]), row)
    for n in range(gram_ref.shape[0]):
        gram_ref[n] = row


def update(ti, amps, ovov, history, inv, parts, copies, capt, across):
    nq = len(parts)
    return pl.pallas_call(
        functools.partial(update_kernel, capt, across, nq),
        in_specs=[SMEM] + [VMEM] * (4 + nq),
        out_specs=[VMEM, VMEM],
        out_shape=[
            jax.ShapeDtypeStruct(amps.shape, BF16),
            jax.ShapeDtypeStruct((copies, 1, LANES), F32),
        ],
        scratch_shapes=[
            pltpu.VMEM(((LIVE2 + capt) * ROWS, LANES), F32),
        ],
        compiler_params=pltpu.CompilerParams(vmem_limit_bytes=24 * 1024 * 1024),
        cost_estimate=pl.CostEstimate(flops=10**8, bytes_accessed=6 * 10**6, transcendentals=0),
        name="update_amps",
    )(ti, amps, ovov, history, inv, *parts)


def finish_kernel(nhist, scale, sums_ref, out_ref):
    total = sums_ref[0]
    for n in range(1, sums_ref.shape[0]):
        total = total + sums_ref[n]
    lane = lax.broadcasted_iota(jnp.int32, total.shape, 1)
    total = jnp.where(lane == nhist, jnp.sqrt(jnp.maximum(total, 0.0)), total) * scale
    out_ref[...] = total[0, : nhist + 1]


def finish(sums, nhist, scale):
    return pl.pallas_call(
        functools.partial(finish_kernel, nhist, scale),
        in_specs=[VMEM],
        out_specs=VMEM,
        out_shape=jax.ShapeDtypeStruct((nhist + 1,), F32),
        name="finish_gram",
    )(sums)


def swap(x, axis, size, step):
    return lax.ppermute(x, axis, [(n, n ^ step) for n in range(size)])


def spread_perm(npair, nq, m):
    return [
        (z * npair + p, ((p // 2) ^ m) * npair + 2 * z + p % 2)
        for z in range(nq)
        for p in range(npair)
    ]


def local(npair, nq, amps, tile_index, ovov, cycle_ints, history, slab, eps_occ, eps_vir):
    occ_dev, jdev, capt, tile_area = amps.shape
    ns = tile_index.shape[0]
    across = cycle_ints.shape[2]
    nhist = history.shape[0]
    assert occ_dev == 1 and jdev == 2 and tile_area == TILE * TILE and capt == 16
    assert ns == npair == 2 * nq
    packed = pack(amps, tile_index, capt, across)
    axes = ("reorder", "pair")
    order = [n // 2 if n % 2 == 0 else nq - 1 - n // 2 for n in range(nq)][::-1]
    turned = [lax.ppermute(packed, axes, spread_perm(npair, nq, m)) for m in order]
    late = lax.optimization_barrier((packed, cycle_ints, tile_index, slab, eps_occ, eps_vir))
    meta, mine, *send = prep(*late[1:3], capt, across, nq)
    inv = denominators(*late[2:], capt, across)
    turned, send, inv = lax.optimization_barrier((turned, send, inv))
    turned = [turned[order.index(m)] for m in range(nq)]
    theirs = [swap(tiles, "pair", npair, 1) for tiles in send]
    sums = multiply("own", meta, [mine], turned, [], nq)
    partial = multiply("sibling", meta, theirs[:1], turned, [sums], nq)
    partial, mine = lax.optimization_barrier((list(partial), mine))
    partial += multiply("both", meta, [mine, theirs[1]], turned, [], nq)
    parts = [
        swap(part, "pair", npair, 2 * e) if e else part
        for e, part in zip(sum_order(nq), partial)
    ]
    new_amps, gram = update(
        tile_index, amps, ovov, history, inv, parts, npair * nq, capt, across
    )
    sums = lax.all_to_all(gram, axes, split_axis=0, concat_axis=0, tiled=True)
    return (new_amps, finish(sums, nhist, 1.0 / (TILE * ns)))


def solution(mesh):
    in_specs = (
        P("pair", "reorder", None, None),
        P(),
        P("pair", "reorder", None, None),
        P("pair", "reorder", None, None, None),
        P(None, "pair", "reorder", None, None),
        P(),
        P(),
        P(),
    )
    out_specs = (P("pair", "reorder", None, None), P())
    body = functools.partial(local, mesh.shape["pair"], mesh.shape["reorder"])
    return jax.shard_map(body, mesh=mesh, in_specs=in_specs, out_specs=out_specs, check_vma=False)
```

```python
import functools

import jax
import jax.numpy as jnp
from jax import lax
from jax.experimental import pallas as pl
from jax.experimental.pallas import tpu as pltpu
from jax.sharding import PartitionSpec as P

TILE = 64
ROWS = 32
LANES = 128
LIVE2 = 24
F32 = jnp.float32
BF16 = jnp.bfloat16
SMEM = pl.BlockSpec(memory_space=pltpu.SMEM)
VMEM = pl.BlockSpec(memory_space=pltpu.VMEM)


def count_live(ti_ref, i, j, capt, dead):
    total = jnp.int32(0)
    for s in range(capt):
        total = total + (ti_ref[i, j, s] < dead).astype(jnp.int32)
    return total


def row_of(idx, across):
    factor = -(-(1 << 17) // across)
    assert all((n * factor) >> 17 == n // across for n in range(across * across + 1))
    return lax.shift_right_logical(idx * factor, 17)


def pack_kernel(capt, across, ti_ref, amps_ref, out_ref, flat_ref, turned_ref):
    first = lax.axis_index("pair")
    second = lax.axis_index("reorder") * 2
    live1 = count_live(ti_ref, first, second + 1, capt, across * across)
    for jj in range(2):
        for p in range(ROWS):
            chunk = amps_ref[0, jj, :, p * LANES : (p + 1) * LANES].astype(F32)
            for g in range(capt // 8):
                start = (jj * capt + g * 8) * ROWS + p
                flat_ref[pl.ds(start, 8, stride=ROWS), :] = chunk[g * 8 : (g + 1) * 8]
    old = lax.broadcasted_iota(jnp.int32, (LANES, LANES), 0)
    new = lax.broadcasted_iota(jnp.int32, (LANES, LANES), 1)
    source = (new // 64) * 64 + (new % 32) * 2 + (new % 64) // 32
    turn = (old == source).astype(F32).astype(BF16)
    turned_ref[...] = jnp.dot(
        flat_ref[...].astype(BF16), turn, preferred_element_type=F32
    ).astype(BF16)
    out_ref[0:capt] = turned_ref[0 : capt * ROWS].reshape(capt, ROWS, LANES)
    out_ref[capt:LIVE2] = jnp.zeros((LIVE2 - capt, ROWS, LANES), BF16)

    def place(s, carry):
        start = pl.multiple_of((capt + s) * ROWS, ROWS)
        out_ref[LIVE2 - live1 + s] = turned_ref[pl.ds(start, ROWS), :]
        return carry

    lax.fori_loop(0, live1, place, 0)


def pack(amps, ti, capt, across):
    return pl.pallas_call(
        functools.partial(pack_kernel, capt, across),
        in_specs=[SMEM, VMEM],
        out_specs=VMEM,
        scratch_shapes=[
            pltpu.VMEM((2 * capt * ROWS, LANES), F32),
            pltpu.VMEM((2 * capt * ROWS, LANES), BF16),
        ],
        out_shape=jax.ShapeDtypeStruct((LIVE2, ROWS, LANES), BF16),
        cost_estimate=pl.CostEstimate(flops=10**8, bytes_accessed=500000, transcendentals=0),
        name="pack_amps",
    )(ti, amps)


def prep_kernel(
    capt, across, nq, nmax, ti_ref, hbm_ref,
    meta_ref, mine_ref, send0_ref, send1_ref, ints_ref, wide_ref, tab_ref, sem,
):
    stride = nmax + 8
    fetch_ints = pltpu.make_async_copy(hbm_ref, ints_ref, sem)
    fetch_ints.start()
    dead = across * across
    me = lax.axis_index("pair")
    sibling = me ^ 1
    plane = lax.axis_index("reorder")
    second = plane * 2

    def build(which, who, k):
        def field(f):
            return (which * 5 + f) * stride

        parity = lax.rem(k, 2)

        def one_first(n, cnt):
            e = jnp.where(n < nq // 2, nq, 2 * nq - 1) - 1 - 2 * n
            i = who ^ (2 * e)
            q = lax.shift_right_logical(who, 1) ^ plane ^ e
            out = n * LIVE2
            for a in range(across + 1):
                tab_ref[a] = -1
            live_in = jnp.int32(0)
            for t in range(capt):
                idx = ti_ref[i, k, t]
                live_in = live_in + (idx < dead).astype(jnp.int32)
                a = row_of(idx, across)
                held = t * 32 + idx - a * across
                old = tab_ref[a]
                tab_ref[a] = jnp.where(old < 0, held, old)
                tab_ref[32 + a] = jnp.where(old < 0, -1, held)
            shift = q * LIVE2 + jnp.where(parity == 1, LIVE2 - live_in, 0)
            live1 = count_live(ti_ref, i, second + 1, capt, dead)
            for jj in range(2):
                for s in range(capt):
                    idx = ti_ref[i, second + jj, s]
                    a = row_of(idx, across)
                    b = idx - a * across
                    h0 = tab_ref[a]
                    h1 = tab_ref[32 + a]
                    hit = (idx < dead) & (h0 >= 0)
                    both = h1 >= 0
                    if which < 2:
                        place = out + (s if jj == 0 else LIVE2 - live1 + s)
                        meta_ref[field(0) + cnt] = place
                        t0 = shift + lax.shift_right_arithmetic(h0, 5)
                        t1 = shift + lax.shift_right_arithmetic(h1, 5)
                        meta_ref[field(1) + cnt] = t0
                        meta_ref[field(2) + cnt] = jnp.where(both, t1, t0)
                    if which != 1:
                        w0 = ((h0 & 31) * across + b) * 2 + jj
                        w1 = ((h1 & 31) * across + b) * 2 + jj
                        meta_ref[field(3) + cnt] = w0
                        meta_ref[field(4) + cnt] = jnp.where(both, w1, -1)
                    cnt = cnt + hit.astype(jnp.int32)
            return cnt

        for group in range(2):
            end = lax.fori_loop(
                group * nq // 2, (group + 1) * nq // 2, one_first, jnp.int32(group * nmax // 2)
            )
            meta_ref[15 * stride + 2 * which + group] = end

    def gather(which, group, tiles_ref, offset):
        first = group * nmax // 2
        total = meta_ref[15 * stride + 2 * which + group]

        def fetch(step, carry):
            for u in range(4):
                e = jnp.minimum(first + step * 4 + u, total - 1)
                for m in range(2):
                    at = jnp.maximum(meta_ref[(which * 5 + 3 + m) * stride + e], 0)
                    wide_ref[2 * u + m] = ints_ref[lax.shift_right_logical(at, 1)].astype(F32)
            for u in range(4):
                e = jnp.minimum(first + step * 4 + u, total - 1)
                for m in range(2):
                    at = meta_ref[(which * 5 + 3 + m) * stride + e]
                    jj = jnp.maximum(at, 0) & 1
                    tile = wide_ref[2 * u + m, pl.ds(jj, ROWS, stride=2), :]
                    if m == 1:
                        tile = jnp.where(at >= 0, tile, 0.0)
                    tiles_ref[e - offset, m * ROWS : (m + 1) * ROWS] = tile.astype(BF16)
            return carry

        lax.fori_loop(0, (total - first + 3) // 4, fetch, 0)

    build(2, sibling, me)
    build(0, me, me)
    build(1, me, sibling)
    fetch_ints.wait()
    for group, send_ref in enumerate((send0_ref, send1_ref)):
        gather(2, group, send_ref, group * nmax // 2)
    for group in range(2):
        gather(0, group, mine_ref, 0)


def prep(cycle_ints, ti, capt, across, nq):
    nmax = nq * LIVE2
    ints = cycle_ints[0].transpose(1, 2, 0, 3).reshape(across, across, 2, ROWS, LANES)
    ints = ints.transpose(0, 1, 3, 2, 4).reshape(across * across, 2 * ROWS, LANES)
    tiles = jax.ShapeDtypeStruct((nmax, 2 * ROWS, LANES), BF16)
    half = jax.ShapeDtypeStruct((nmax // 2, 2 * ROWS, LANES), BF16)
    return pl.pallas_call(
        functools.partial(prep_kernel, capt, across, nq, nmax),
        in_specs=[SMEM, pl.BlockSpec(memory_space=pltpu.HBM)],
        out_specs=[SMEM, VMEM, VMEM, VMEM],
        scratch_shapes=[
            pltpu.VMEM(ints.shape, BF16),
            pltpu.VMEM((8, 2 * ROWS, LANES), F32),
            pltpu.SMEM((64,), jnp.int32),
            pltpu.SemaphoreType.DMA,
        ],
        out_shape=[
            jax.ShapeDtypeStruct((15 * (nmax + 8) + 8,), jnp.int32), tiles, half, half
        ],
        compiler_params=pltpu.CompilerParams(vmem_limit_bytes=50 * 1024 * 1024),
        cost_estimate=pl.CostEstimate(flops=10**9, bytes_accessed=40 * 10**6, transcendentals=0),
        name="prep_integrals",
    )(ti, ints)


def denom_kernel(capt, across, ti_ref, slab_ref, occ_ref, vir_ref, inv_ref, row_ref, col_ref):
    first = lax.axis_index("pair")
    second = lax.axis_index("reorder") * 2
    occ_i = occ_ref[slab_ref[first]]
    low = lax.broadcasted_iota(jnp.int32, (8, LANES), 1) < 64
    for jj in range(2):
        for s in range(capt):
            idx = ti_ref[first, second + jj, s]
            row = row_of(idx, across)
            a = jnp.minimum(row, across - 1)
            b = idx - row * across
            row_ref[jj * capt + s] = vir_ref[a]
            col_ref[jj * capt + s] = vir_ref[b]
    for jj in range(2):
        occ = occ_i + occ_ref[slab_ref[second + jj]]
        for g in range(capt // 8):
            here = pl.ds(jj * capt + g * 8, 8)
            rows = occ - row_ref[here]
            col = col_ref[here]
            cols = jnp.concatenate([col, col], axis=1)
            for p in range(ROWS):
                even = jnp.broadcast_to(rows[:, 2 * p : 2 * p + 1], (8, LANES))
                odd = jnp.broadcast_to(rows[:, 2 * p + 1 : 2 * p + 2], (8, LANES))
                inv_ref[jj, g * 8 : (g + 1) * 8, p * LANES : (p + 1) * LANES] = 1.0 / (
                    jnp.where(low, even, odd) - cols
                )


def denominators(ti, slab, eps_occ, eps_vir, capt, across):
    return pl.pallas_call(
        functools.partial(denom_kernel, capt, across),
        in_specs=[SMEM, SMEM, SMEM, VMEM],
        out_specs=VMEM,
        scratch_shapes=[pltpu.VMEM((2 * capt, 64), F32)] * 2,
        out_shape=jax.ShapeDtypeStruct((2, capt, TILE * TILE), F32),
        cost_estimate=pl.CostEstimate(flops=1000, bytes_accessed=1000, transcendentals=0),
        name="denominators",
    )(ti, slab, eps_occ, eps_vir.reshape(across, 64))


def sum_order(nq):
    return [e for e in range(nq - 1, -1, -2)] + [e for e in range(nq - 2, -1, -2)]


def multiply_kernel(part, nq, nmax, unroll, meta_ref, *refs):
    half = nmax // 2
    stride = nmax + 8
    group = 1 if part == "both" else 0
    tiles = {"own": 1, "sibling": 1, "both": 2}[part]
    tiles_refs, amps_refs, refs = refs[:tiles], refs[tiles : tiles + nq], refs[tiles + nq :]
    if part == "own":
        sum_ref, amps_ref = refs
        work = [(0, tiles_refs[0], 0)]
    elif part == "sibling":
        own_ref, out_refs, (amps_ref, sum_ref) = refs[0], refs[1:-2], refs[-2:]
        work = [(1, tiles_refs[0], 0)]
    else:
        out_refs, (amps_ref, sum_ref) = refs[:-2], refs[-2:]
        work = [(0, tiles_refs[0], 0), (1, tiles_refs[1], half)]
    if part == "sibling":
        sum_ref[0:half] = own_ref[0:half]
    else:
        sum_ref[...] = jnp.zeros(sum_ref.shape, F32)
    for q in range(nq):
        amps_ref[q * LIVE2 : (q + 1) * LIVE2] = amps_refs[q][...]
    low = lax.broadcasted_iota(jnp.int32, (ROWS, LANES), 1) < 64

    def spread(w):
        w = w.astype(F32)
        r = pltpu.roll(w, 64, 1)
        zero = jnp.zeros_like(w)
        parts = [
            jnp.where(low, w, zero),
            jnp.where(low, r, zero),
            jnp.where(low, zero, r),
            jnp.where(low, zero, w),
        ]
        return jnp.concatenate(parts, axis=0).astype(BF16)

    first = group * half
    for which, tiles_ref, offset in work:
        total = meta_ref[15 * stride + 2 * which + group]

        def several(step, carry):
            results = []
            for u in range(unroll):
                e = jnp.minimum(first + step * unroll + u, total - 1)
                at = which * 5 * stride + e
                left = jnp.concatenate(
                    [amps_ref[meta_ref[stride + at]], amps_ref[meta_ref[2 * stride + at]]],
                    axis=1,
                )
                right = jnp.concatenate(
                    [
                        spread(tiles_ref[e - offset, 0:ROWS]),
                        spread(tiles_ref[e - offset, ROWS : 2 * ROWS]),
                    ],
                    axis=0,
                )
                inside = first + step * unroll + u < total
                place = jnp.where(inside, meta_ref[at] - first, half)
                results.append((place, jnp.dot(left, right, preferred_element_type=F32)))
            for place, value in results:
                if which == 0:
                    sum_ref[place] = value
                else:
                    sum_ref[place] += value
            return carry

        lax.fori_loop(0, (total - first + unroll - 1) // unroll, several, 0)
    if part != "own":
        for n in range(nq // 2):
            out_refs[n][...] = sum_ref[n * LIVE2 : (n + 1) * LIVE2].astype(BF16)


def multiply(part, meta, tiles, amps, sums, nq):
    nmax = nq * LIVE2
    scratch = [pltpu.VMEM((nmax, ROWS, LANES), BF16)]
    sum_shape = (nmax // 2 + 1, ROWS, LANES)
    if part == "own":
        out = jax.ShapeDtypeStruct(sum_shape, F32)
    else:
        out = [jax.ShapeDtypeStruct((LIVE2, ROWS, LANES), BF16)] * (nq // 2)
        scratch.append(pltpu.VMEM(sum_shape, F32))
    return pl.pallas_call(
        functools.partial(multiply_kernel, part, nq, nmax, 8),
        in_specs=[SMEM] + [VMEM] * (len(tiles) + len(amps) + len(sums)),
        out_specs=jax.tree.map(lambda _: VMEM, out),
        out_shape=out,
        scratch_shapes=scratch,
        compiler_params=pltpu.CompilerParams(vmem_limit_bytes=24 * 1024 * 1024),
        cost_estimate=pl.CostEstimate(flops=10**9, bytes_accessed=6 * 10**6, transcendentals=0),
        name="multiply_" + part,
    )(meta, *tiles, *amps, *sums)


def update_kernel(
    capt, across, nq, ti_ref, amps_ref, ovov_ref, hist_ref, inv_ref, *refs
):
    part_refs, (new_ref, gram_ref, sum_ref) = refs[:nq], refs[nq:]
    nhist = hist_ref.shape[0]
    first = lax.axis_index("pair")
    second = lax.axis_index("reorder") * 2

    def add(s, carry):
        acc = part_refs[0][s].astype(F32)
        for part_ref in part_refs[1:]:
            acc = acc + part_ref[s].astype(F32)
        sum_ref[pl.ds(pl.multiple_of(s * ROWS, ROWS), ROWS), :] = acc
        return carry

    lax.fori_loop(0, LIVE2, add, 0, unroll=4)
    slot = lax.broadcasted_iota(jnp.int32, (8, LANES), 0)
    accs = [jnp.zeros((8, LANES), F32) for _ in range(nhist + 1)]
    for jj in range(2):
        count = count_live(ti_ref, first, second + jj, capt, across * across)
        start = 0 if jj == 0 else (LIVE2 - count) * ROWS
        for g in range(capt // 8):
            alive = slot + g * 8 < count
            rows = slice(g * 8, (g + 1) * 8)

            def chunk(p, accs):
                here = pl.ds(pl.multiple_of(p * LANES, LANES), LANES)
                cycle = sum_ref[pl.ds(start + g * 8 * ROWS + p, 8, stride=ROWS), :]
                resid = jnp.where(alive, ovov_ref[0, jj, rows, here].astype(F32) + cycle, 0.0)
                moved = amps_ref[0, jj, rows, here].astype(F32) + resid * inv_ref[jj, rows, here]
                new_ref[0, jj, rows, here] = jnp.where(alive, moved, 0.0).astype(BF16)
                out = [
                    accs[m] + hist_ref[m, 0, jj, rows, here].astype(F32) * resid
                    for m in range(nhist)
                ]
                out.append(accs[nhist] + resid * resid)
                return out

            accs = lax.fori_loop(0, ROWS, chunk, accs, unroll=8)
    lane = lax.broadcasted_iota(jnp.int32, (1, LANES), 1)
    row = jnp.zeros((1, LANES), F32)
    for m in range(nhist + 1):
        row = jnp.where(lane == m, jnp.sum(accs[m]), row)
    for n in range(gram_ref.shape[0]):
        gram_ref[n] = row


def update(ti, amps, ovov, history, inv, parts, copies, capt, across):
    nq = len(parts)
    return pl.pallas_call(
        functools.partial(update_kernel, capt, across, nq),
        in_specs=[SMEM] + [VMEM] * (4 + nq),
        out_specs=[VMEM, VMEM],
        out_shape=[
            jax.ShapeDtypeStruct(amps.shape, BF16),
            jax.ShapeDtypeStruct((copies, 1, LANES), F32),
        ],
        scratch_shapes=[
            pltpu.VMEM(((LIVE2 + capt) * ROWS, LANES), F32),
        ],
        compiler_params=pltpu.CompilerParams(vmem_limit_bytes=24 * 1024 * 1024),
        cost_estimate=pl.CostEstimate(flops=10**8, bytes_accessed=6 * 10**6, transcendentals=0),
        name="update_amps",
    )(ti, amps, ovov, history, inv, *parts)


def finish_kernel(nhist, scale, sums_ref, out_ref):
    total = sums_ref[0]
    for n in range(1, sums_ref.shape[0]):
        total = total + sums_ref[n]
    lane = lax.broadcasted_iota(jnp.int32, total.shape, 1)
    total = jnp.where(lane == nhist, jnp.sqrt(jnp.maximum(total, 0.0)), total) * scale
    out_ref[...] = total[0, : nhist + 1]


def finish(sums, nhist, scale):
    return pl.pallas_call(
        functools.partial(finish_kernel, nhist, scale),
        in_specs=[VMEM],
        out_specs=VMEM,
        out_shape=jax.ShapeDtypeStruct((nhist + 1,), F32),
        name="finish_gram",
    )(sums)


def swap(x, axis, size, step):
    return lax.ppermute(x, axis, [(n, n ^ step) for n in range(size)])


def spread_perm(npair, nq, m):
    return [
        (z * npair + p, ((p // 2) ^ m) * npair + 2 * z + p % 2)
        for z in range(nq)
        for p in range(npair)
    ]


def local(npair, nq, amps, tile_index, ovov, cycle_ints, history, slab, eps_occ, eps_vir):
    occ_dev, jdev, capt, tile_area = amps.shape
    ns = tile_index.shape[0]
    across = cycle_ints.shape[2]
    nhist = history.shape[0]
    assert occ_dev == 1 and jdev == 2 and tile_area == TILE * TILE and capt == 16
    assert ns == npair == 2 * nq
    packed = pack(amps, tile_index, capt, across)
    axes = ("reorder", "pair")
    order = [n // 2 if n % 2 == 0 else nq - 1 - n // 2 for n in range(nq)][::-1]
    turned = [lax.ppermute(packed, axes, spread_perm(npair, nq, m)) for m in order]
    late = lax.optimization_barrier((packed, cycle_ints, tile_index))
    meta, mine, *send = prep(*late[1:], capt, across, nq)
    turned, send = lax.optimization_barrier((turned, send))
    turned = [turned[order.index(m)] for m in range(nq)]
    theirs = [swap(tiles, "pair", npair, 1) for tiles in send]
    sums = multiply("own", meta, [mine], turned, [], nq)
    partial = multiply("sibling", meta, theirs[:1], turned, [sums], nq)
    partial, mine = lax.optimization_barrier((list(partial), mine))
    partial += multiply("both", meta, [mine, theirs[1]], turned, [], nq)
    late = lax.optimization_barrier((partial[-1], tile_index, slab, eps_occ, eps_vir))
    inv = denominators(*late[1:], capt, across)
    parts = [
        swap(part, "pair", npair, 2 * e) if e else part
        for e, part in zip(sum_order(nq), partial)
    ]
    new_amps, gram = update(
        tile_index, amps, ovov, history, inv, parts, npair * nq, capt, across
    )
    sums = lax.all_to_all(gram, axes, split_axis=0, concat_axis=0, tiled=True)
    return (new_amps, finish(sums, nhist, 1.0 / (TILE * ns)))


def solution(mesh):
    in_specs = (
        P("pair", "reorder", None, None),
        P(),
        P("pair", "reorder", None, None),
        P("pair", "reorder", None, None, None),
        P(None, "pair", "reorder", None, None),
        P(),
        P(),
        P(),
    )
    out_specs = (P("pair", "reorder", None, None), P())
    body = functools.partial(local, mesh.shape["pair"], mesh.shape["reorder"])
    return jax.shard_map(body, mesh=mesh, in_specs=in_specs, out_specs=out_specs, check_vma=False)
```
